256 devices in a mesh: chan: 16 (over x, z_lo, core), depth: 16 (over z_hi, y).
Axes of the slice: x: 4, y: 4, z: 8 (z_hi: 4, z_lo: 2; z = z_hi * 2 + z_lo), core: 2. Of those that a mesh axis runs over, the one named last changes fastest.
Arguments:
- features: bfloat16 [512, 32, 4096], P('chan', 'depth'), may hold values from -6 to 6
- kernel: bfloat16 [512, 27, 512], P('chan'), may hold values from -0.0625 to 0.0625
- cotangent: bfloat16 [512, 16, 1024], P('chan', 'depth'), may hold values from -6 to 6
Outputs:
- response: bfloat16 [512, 16, 1024], P('chan', 'depth')
- feature_grad: bfloat16 [512, 32, 4096], P('chan', 'depth')
- kernel_grad: float32 [512, 27, 512], P('chan')
The draws below stay inside these ranges and needn't reach their ends.
All inputs are finite; a program needn't handle non-finite values.
Results may differ from the reference program's by a relative error of at most 0.001.
Values may be sent and summed in bfloat16 or wider, within the bound.
A program may use at most 128 MiB of HBM per device.

```python
import jax
import jax.numpy as jnp
from jax import lax

CIN = 512
COUT = 512
H = 64
W = 64
TAPS = 27
DEPTH = 32
DOUT = 16
HW = 4096
HWO = 1024
OUT_POSITIONS = 16384


def raised(entries, key, source, target, parts, factor):
    owner, partner = [(jnp.arange(entries.shape[axis_at]) // (entries.shape[axis_at] // parts)).reshape([-1 if axis == axis_at else 1 for axis in range(entries.ndim)]) for axis_at in (source, target)]
    chosen = jax.random.permutation(key, parts)[partner]
    strong = (owner == chosen) | (owner == (partner + parts // 2) % parts)
    return jnp.where(strong, factor * entries, entries)


def steps_of(own_key, extent, cuts, least, largest):
    def one(position, blocks):
        heights = jax.random.uniform(jax.random.fold_in(jax.random.fold_in(own_key, 6), position), (blocks,), jnp.float32, least / len(cuts), largest / len(cuts))
        return jnp.repeat(jnp.exp(heights), extent[position] // blocks).reshape((-1,) + (1,) * (len(extent) - position - 1))

    factor_of = one(*cuts[0])
    for cut in cuts[1:]:
        factor_of = factor_of * one(*cut)
    return factor_of


def normal_values(rng, extent, spread, reach, split=(), held_as=jnp.bfloat16):
    array = spread * jax.random.normal(rng, extent, jnp.float32)
    if split:
        array = array * steps_of(rng, extent, split, -0.22, 0.18)
    return jnp.clip(array, -reach, reach).astype(held_as)


def heavy_noise(stream_key, dims, width, bound, cuts, heavy, held_as=jnp.bfloat16):
    values = width * jax.random.normal(stream_key, dims, jnp.float32)
    if cuts:
        values = values * steps_of(stream_key, dims, cuts, -0.22, 0.18)
    return jnp.clip(raised(values, jax.random.fold_in(stream_key, 3), *heavy), -bound, bound).astype(held_as)


def setup_inputs(seed: int = 0) -> dict:
    seeds = jax.random.split(jax.random.key(seed), 4)
    return {
        "features": normal_values(seeds[0], (CIN, DEPTH, HW), 1.0, 6.0, ((0, 16), (1, 16))),
        "kernel": heavy_noise(seeds[1], (CIN, TAPS, COUT), (TAPS * CIN) ** -0.5, 0.0625, ((0, 16),), (0, 2, 16, 2.0)),
        "cotangent": normal_values(seeds[2], (COUT, DOUT, HWO), 1.0, 6.0, ((0, 16), (1, 16))),
    }


def convolve(field, weights):
    return lax.conv_general_dilated(field, weights, (2, 2, 2), ((1, 1), (1, 1), (1, 1)), dimension_numbers=('NCDHW', 'OIDHW', 'NCDHW'), precision=lax.Precision.HIGHEST)

def reference(features, kernel, cotangent):
    field = features.astype(jnp.float32).reshape(1, CIN, DEPTH, H, W)
    weights = kernel.astype(jnp.float32).reshape(CIN, 3, 3, 3, COUT).transpose(4, 0, 1, 2, 3)
    result, pullback = jax.vjp(convolve, field, weights)
    upstream = cotangent.astype(jnp.float32).reshape(1, COUT, DOUT, H // 2, W // 2)
    field_grad, weight_grad = pullback(upstream)
    response = result.reshape(COUT, DOUT, HWO).astype(jnp.bfloat16)
    feature_grad = field_grad.reshape(CIN, DEPTH, HW).astype(jnp.bfloat16)
    kernel_grad = weight_grad.transpose(1, 2, 3, 4, 0).reshape(CIN, TAPS, COUT) * float(OUT_POSITIONS) ** (-0.5)
    return (response, feature_grad, kernel_grad.astype(jnp.float32))
```

```python
import jax
import jax.numpy as jnp
from jax import lax
from jax.experimental import pallas as pl
from jax.experimental.pallas import tpu as pltpu
from jax.sharding import PartitionSpec as P

BF16 = jnp.bfloat16
F32 = jnp.float32
MESH = pl.DeviceIdType.MESH
SPAN = 250.0
MESSAGES = 96


def near(i):
    return i + 1 - 2 * (i % 2)


def far(i):
    return 3 - i


def ring_order(half):
    return (near, far) if half == 0 else (far, near)


def bound_of(values):
    rows, lanes = values.shape
    top = jnp.max(jnp.abs(values).reshape(rows // 16, 16, lanes), axis=0)
    return jnp.maximum(top, 1e-30).astype(BF16).astype(F32)


def encode(values, bound):
    rows, lanes = values.shape
    blocks = values.reshape(rows // 16, 16, lanes)
    code = jnp.exp2(jnp.abs(blocks) * (SPAN / bound)[None] - SPAN / 2)
    return jnp.where(blocks < 0, -code, code).reshape(rows, lanes).astype(BF16)


def decode(code, bound, scale=1.0):
    rows, lanes = code.shape
    blocks = code.astype(F32).reshape(rows // 16, 16, lanes)
    size = (jnp.log2(jnp.abs(blocks)) + SPAN / 2) * (bound * (scale / SPAN))[None]
    return jnp.where(blocks < 0, -size, size).reshape(rows, lanes)


def dot(a, b, dims):
    return lax.dot_general(a, b, (dims, ((), ())), preferred_element_type=F32)


def kernel(
    feat, kern, cot, resp, fgrad, kgrad,
    perm, patches, cells_out, cells_in, gathered, terms, spread,
    part, run, sy1, ry1, sy2, ry2, sz1, rz1, sz2, rz2, codes,
    sc, rc, sx1, rx1, sx2, rx2, sz, rz, send_sem, recv_sem,
):
    chan = lax.axis_index("chan")
    depth = lax.axis_index("depth")
    x, zl, core = chan // 4, (chan // 2) % 2, chan % 2
    zh, y = depth // 4, depth % 4
    to_core = (chan + 1 - 2 * core, depth)
    to_zl = (4 * x + 2 * (1 - zl) + core, depth)
    up = (chan, (depth + 1) % 16)
    down = (chan, (depth + 15) % 16)

    def to_x(step):
        return (4 * step(x) + 2 * zl + core, depth)

    def to_y(step):
        return (chan, 4 * zh + step(y))

    def to_zh(step):
        return (chan, 4 * step(zh) + y)

    partners = (
        to_core, to_zl, up, down,
        to_x(near), to_x(far), to_y(near), to_y(far), to_zh(near), to_zh(far),
    )
    barrier = pltpu.get_barrier_semaphore()
    for partner in partners:
        pl.semaphore_signal(barrier, inc=1, device_id=partner, device_id_type=MESH)
    pl.semaphore_wait(barrier, len(partners))

    copies = []

    def send(src, dst, device):
        at = len(copies)
        copy = pltpu.make_async_remote_copy(
            src_ref=src, dst_ref=dst, send_sem=send_sem.at[at], recv_sem=recv_sem.at[at],
            device_id=device, device_id_type=MESH,
        )
        copy.start()
        copies.append(copy)
        return copy

    moves = [{}, {}]

    def gather_z(j, src):
        moves[j]["z"] = send(src, gathered.at[j, x, zl, core], to_zl)

    def gather_x(j):
        m = moves[j]
        m["z"].wait_recv()
        pair = gathered.at[j, x, :, core]
        m["near"] = send(pair, pair, to_x(near))
        m["far"] = send(pair, pair, to_x(far))
        m["own_core"] = send(pair, pair, to_core)

    def gather_opposite(j):
        m = moves[j]
        m["near"].wait_recv()
        first = gathered.at[j, near(x), :, core, 0:16]
        m["opp0"] = send(first, first, to_x(far))
        block = gathered.at[j, near(x), :, core]
        m["near_core"] = send(block, block, to_core)
        m["far"].wait_recv()
        second = gathered.at[j, far(x), :, core, 16:32]
        m["opp1"] = send(second, second, to_x(near))
        block = gathered.at[j, far(x), :, core]
        m["far_core"] = send(block, block, to_core)

    def gather_last(j):
        m = moves[j]
        m["opp0"].wait_recv()
        m["opp1"].wait_recv()
        block = gathered.at[j, near(far(x)), :, core]
        m["opp_core"] = send(block, block, to_core)

    def gather_wait(j, group):
        names = ("own_core", "near_core") if group == 0 else ("far_core", "opp_core")
        for name in names:
            moves[j][name].wait_recv()

    gathered[0, x, zl, core] = cot[...]
    gather_z(0, cot)
    halo_cot = send(cot, gathered.at[1, x, zl, core], down)

    lane_in = lax.broadcasted_iota(jnp.int32, (512, 512), 0)
    lane_out = lax.broadcasted_iota(jnp.int32, (512, 512), 1)
    target = (
        ((lane_in >> 6) & 1) * 256 + (lane_in & 1) * 128
        + (lane_in >> 7) * 32 + ((lane_in & 63) >> 1)
    )
    perm[...] = jnp.where(target == lane_out, 1.0, 0.0).astype(BF16)

    def split_cells(plane):
        rows = feat[:, plane, :]
        stacked = jnp.concatenate([rows[:, 512 * k : 512 * k + 512] for k in range(8)], axis=0)
        sorted_cells = dot(stacked, perm[...], ((1,), (0,))).astype(BF16)
        return [
            jnp.concatenate(
                [sorted_cells[32 * k : 32 * k + 32, 128 * q : 128 * q + 128] for k in range(8)],
                axis=1,
            )
            for q in range(4)
        ]

    lane = lax.broadcasted_iota(jnp.int32, (32, 1024), 1)
    not_first_col = jnp.where((lane & 31) > 0, 1.0, 0.0).astype(BF16)
    not_first_row = jnp.where(lane >= 32, 1.0, 0.0).astype(BF16)

    def right(v):
        return pltpu.roll(v, 1, 1) * not_first_col

    def lower(v):
        return pltpu.roll(v, 32, 1) * not_first_row

    def lay_patches(a, cells):
        ee, eo, oe, oo = cells
        eo_r, oo_r = right(eo), right(oo)
        rows = (
            (lower(oo_r), lower(oe), lower(oo)),
            (eo_r, ee, eo),
            (oo_r, oe, oo),
        )
        for b in range(3):
            for c in range(3):
                at = (9 * a + 3 * b + c) * 32
                patches[at : at + 32] = rows[b][c]

    odd = split_cells(1)
    for q in range(4):
        cells_out[q] = odd[q]
    halo_feat = send(cells_out, cells_in, up)
    gather_x(0)
    lay_patches(2, odd)
    lay_patches(1, split_cells(0))
    patches[864:896] = jnp.zeros((32, 1024), BF16)
    gather_opposite(0)
    halo_cot.wait_recv()
    gather_z(1, gathered.at[1, x, zl, core])
    halo_feat.wait_recv()
    has_below = jnp.where(depth > 0, 1.0, 0.0).astype(BF16)
    lay_patches(0, [cells_in[q] * has_below for q in range(4)])

    grads = {}

    def pair_at(group):
        return x // 2 if group == 0 else 1 - x // 2

    def grad_terms(g):
        weights = gathered[0, pl.ds(2 * pair_at(g), 2)].reshape(256, 1024)
        for h in (1, 0):
            first, second = ring_order(h)
            value = dot(patches[448 * h : 448 * h + 448], weights, ((1,), (1,)))
            for q in range(4):
                part[g, h, q, 0:112] = value[112 * q : 112 * q + 112]
            bound = bound_of(value)
            run[g, h] = bound
            sy1[g, h, 0:112] = encode(part[g, h, first(y), 0:112], bound)
            sy1[g, h, 112:224] = encode(part[g, h, second(first(y)), 0:112], bound)
            sy1[g, h, 224:240] = bound.astype(BF16)
            grads[g, h] = [send(sy1.at[g, h], ry1.at[g, h], to_y(first))]

    def merge_bound(g, h, other):
        bound = jnp.maximum(run[g, h], other)
        run[g, h] = bound
        return bound

    def grad_y2(g):
        for h in (1, 0):
            first, second = ring_order(h)
            grads[g, h][0].wait_recv()
            other = ry1[g, h, 224:240].astype(F32)
            bound = merge_bound(g, h, other)
            part[g, h, second(y), 0:112] += decode(ry1[g, h, 112:224], other)
            sy2[g, h, 0:112] = encode(part[g, h, second(y), 0:112], 2 * bound)
            sy2[g, h, 112:128] = bound.astype(BF16)
            grads[g, h] = [send(sy2.at[g, h], ry2.at[g, h], to_y(second))]
            part[g, h, y, 0:112] += decode(ry1[g, h, 0:112], other)

    def cells(i):
        return pl.ds(pl.multiple_of(32 * i, 32), 32)

    def grad_z1(g):
        for h in (1, 0):
            first, second = ring_order(h)
            grads[g, h][0].wait_recv()
            other = ry2[g, h, 112:128].astype(F32)
            bound = merge_bound(g, h, other)
            part[g, h, y, 0:112] += decode(ry2[g, h, 0:112], 2 * other)
            part[g, h, y, 112:128] = jnp.zeros((16, 256), F32)
            sz1[g, h, 0:32] = encode(part[g, h, y, cells(first(zh))], 4 * bound)
            sz1[g, h, 32:64] = encode(part[g, h, y, cells(second(first(zh)))], 4 * bound)
            sz1[g, h, 64:80] = bound.astype(BF16)
            grads[g, h] = [send(sz1.at[g, h], rz1.at[g, h], to_zh(first))]

    def grad_z2(g):
        for h in (1, 0):
            first, second = ring_order(h)
            grads[g, h][0].wait_recv()
            other = rz1[g, h, 64:80].astype(F32)
            bound = merge_bound(g, h, other)
            part[g, h, y, cells(second(zh))] += decode(rz1[g, h, 32:64], 4 * other)
            sz2[g, h, 0:32] = encode(part[g, h, y, cells(second(zh))], 8 * bound)
            sz2[g, h, 32:48] = bound.astype(BF16)
            grads[g, h] = [send(sz2.at[g, h], rz2.at[g, h], to_zh(second))]
            part[g, h, y, cells(zh)] += decode(rz1[g, h, 0:32], 4 * other)

    def back_z1(g):
        for h in (1, 0):
            first, second = ring_order(h)
            grads[g, h][0].wait_recv()
            other = rz2[g, h, 32:48].astype(F32)
            bound = merge_bound(g, h, other)
            total = part[g, h, y, cells(zh)] + decode(rz2[g, h, 0:32], 8 * other)
            codes[g, h, y, cells(zh)] = encode(total, 16 * bound)
            own = codes.at[g, h, y, cells(zh)]
            grads[g, h] = [send(own, own, to_zh(second)), send(own, own, to_zh(first))]

    def back_z2(g):
        for h in (1, 0):
            first, second = ring_order(h)
            grads[g, h][0].wait_recv()
            block = codes.at[g, h, y, cells(second(zh))]
            grads[g, h][0] = send(block, block, to_zh(first))

    def back_y1(g):
        for h in (1, 0):
            first, second = ring_order(h)
            grads[g, h][0].wait_recv()
            grads[g, h][1].wait_recv()
            block = codes.at[g, h, y, 0:112]
            grads[g, h] = [send(block, block, to_y(second)), send(block, block, to_y(first))]

    def back_y2(g):
        for h in (1, 0):
            first, second = ring_order(h)
            grads[g, h][0].wait_recv()
            block = codes.at[g, h, second(y), 0:112]
            grads[g, h][0] = send(block, block, to_y(first))

    def grad_result(g):
        lanes = pl.ds(pl.multiple_of(256 * pair_at(g), 256), 256)
        for h in (1, 0):
            grads[g, h][0].wait_recv()
            grads[g, h][1].wait_recv()
            for q in range(4):
                at = 448 * h + 112 * q
                count = min(112, 864 - at)
                kgrad[at : at + count, lanes] = decode(
                    codes[g, h, q, 0:count], 16 * run[g, h], 1.0 / 128
                )

    sums = {}

    def resp_terms():
        for i in range(4):
            value = dot(kern[:, 128 * i : 128 * i + 128], patches[0:864], ((0,), (0,)))
            terms[i] = value.reshape(2, 2, 32, 1024)
        bound = bound_of(terms[:, :, 1 - core].reshape(256, 1024))
        for i in range(4):
            for j in range(2):
                at = 64 * i + 32 * j
                sc[at : at + 32] = encode(terms[i, j, 1 - core], bound)
        sc[256:272] = bound.astype(BF16)
        sums["core"] = send(sc, rc, to_core)

    def resp_x1():
        sums["core"].wait_recv()
        other = rc[256:272].astype(F32)
        for i in range(4):
            for j in range(2):
                at = 64 * i + 32 * j
                terms[i, j, core] += decode(rc[at : at + 32], other)
        for h in range(2):
            first, second = ring_order(h)
            lanes = slice(512 * h, 512 * h + 512)
            blocks = [
                terms[i, j, core, :, lanes] for i in (first(x), second(first(x))) for j in range(2)
            ]
            value = jnp.concatenate(blocks, axis=0)
            bound = bound_of(value)
            sx1[h, 0:128] = encode(value, bound)
            sx1[h, 128:144] = bound.astype(BF16)
            sums["x1", h] = send(sx1.at[h], rx1.at[h], to_x(first))

    def resp_x2():
        for h in range(2):
            first, second = ring_order(h)
            lanes = slice(512 * h, 512 * h + 512)
            sums["x1", h].wait_recv()
            other = rx1[h, 128:144].astype(F32)
            for n, i in enumerate((x, second(x))):
                for j in range(2):
                    at = 64 * n + 32 * j
                    terms[i, j, core, :, lanes] += decode(rx1[h, at : at + 32], other)
            value = jnp.concatenate(
                [terms[second(x), j, core, :, lanes] for j in range(2)], axis=0
            )
            bound = bound_of(value)
            sx2[h, 0:64] = encode(value, bound)
            sx2[h, 64:80] = bound.astype(BF16)
            sums["x2", h] = send(sx2.at[h], rx2.at[h], to_x(second))

    def resp_z():
        for h in range(2):
            lanes = slice(512 * h, 512 * h + 512)
            sums["x2", h].wait_recv()
            other = rx2[h, 64:80].astype(F32)
            for j in range(2):
                terms[x, j, core, :, lanes] += decode(rx2[h, 32 * j : 32 * j + 32], other)
        value = terms[x, 1 - zl, core]
        bound = bound_of(value)
        sz[0:32] = encode(value, bound)
        sz[32:48] = bound.astype(BF16)
        sums["z"] = send(sz, rz, to_zl)

    def resp_result():
        sums["z"].wait_recv()
        total = terms[x, zl, core] + decode(rz[0:32], rz[32:48].astype(F32))
        resp[...] = total.astype(BF16)

    not_last_col = jnp.where((lane & 31) < 31, 1.0, 0.0)
    not_last_row = jnp.where(lane < 992, 1.0, 0.0)

    def left(v):
        return pltpu.roll(v, 1023, 1) * not_last_col

    def upper(v):
        return pltpu.roll(v, 992, 1) * not_last_row

    def join_cells(plane):
        def tap(b, c):
            at = (3 * b + c) * 32
            return spread[at : at + 32]

        cells = [
            tap(1, 1),
            tap(1, 2) + left(tap(1, 0)),
            tap(2, 1) + upper(tap(0, 1)),
            tap(2, 2) + left(tap(2, 0)) + upper(tap(0, 2) + left(tap(0, 0))),
        ]
        cells = [v.astype(BF16) for v in cells]
        stacked = jnp.concatenate(
            [
                jnp.concatenate([v[:, 128 * k : 128 * k + 128] for v in cells], axis=1)
                for k in range(8)
            ],
            axis=0,
        )
        rows = dot(stacked, perm[...], ((1,), (1,))).astype(BF16)
        for k in range(8):
            fgrad[32 * plane : 32 * plane + 32, 512 * k : 512 * k + 512] = rows[
                32 * k : 32 * k + 32
            ]

    def feature_even():
        cots = gathered[0].reshape(512, 1024)
        spread[...] = dot(kern[288:576], cots, ((1,), (0,)))
        join_cells(0)

    def feature_odd():
        has_above = jnp.where(depth < 15, 1.0, 0.0)
        spread[...] = dot(kern[0:288], gathered[1].reshape(512, 1024), ((1,), (0,))) * has_above
        spread[...] += dot(kern[576:864], gathered[0].reshape(512, 1024), ((1,), (0,)))
        join_cells(1)

    gather_wait(0, 0)
    grad_terms(0)
    gather_last(0)
    resp_terms()
    gather_wait(0, 1)
    grad_terms(1)
    gather_x(1)
    grad_y2(0)
    resp_x1()
    grad_y2(1)
    gather_opposite(1)
    grad_z1(0)
    resp_x2()
    grad_z1(1)
    grad_z2(0)
    gather_last(1)
    grad_z2(1)
    back_z1(0)
    resp_z()
    back_z1(1)
    back_z2(0)
    feature_even()
    back_z2(1)
    back_y1(0)
    back_y1(1)
    resp_result()
    gather_wait(1, 0)
    gather_wait(1, 1)
    feature_odd()
    back_y2(0)
    back_y2(1)
    grad_result(0)
    grad_result(1)
    for copy in copies:
        copy.wait_send()


def on_device(features, kernel_block, cotangent):
    kern = kernel_block.transpose(1, 0, 2).reshape(864, 512)
    cot = cotangent.reshape(32, 1024)
    shape = jax.ShapeDtypeStruct
    vmem = pl.BlockSpec(memory_space=pltpu.VMEM)
    resp, fgrad, kgrad = pl.pallas_call(
        kernel,
        out_shape=(shape((32, 1024), BF16), shape((64, 4096), BF16), shape((864, 512), F32)),
        in_specs=[vmem] * 3,
        out_specs=(vmem,) * 3,
        scratch_shapes=[
            pltpu.VMEM((512, 512), BF16),
            pltpu.VMEM((896, 1024), BF16),
            pltpu.VMEM((4, 32, 1024), BF16),
            pltpu.VMEM((4, 32, 1024), BF16),
            pltpu.VMEM((2, 4, 2, 2, 32, 1024), BF16),
            pltpu.VMEM((4, 2, 2, 32, 1024), F32),
            pltpu.VMEM((288, 1024), F32),
            pltpu.VMEM((2, 2, 4, 128, 256), F32),
            pltpu.VMEM((2, 2, 16, 256), F32),
        ]
        + [
            pltpu.VMEM((2, 2, rows, 256), BF16)
            for rows in (240, 240, 128, 128, 80, 80, 48, 48)
        ]
        + [
            pltpu.VMEM((2, 2, 4, 128, 256), BF16),
            pltpu.VMEM((272, 1024), BF16),
            pltpu.VMEM((272, 1024), BF16),
            pltpu.VMEM((2, 144, 512), BF16),
            pltpu.VMEM((2, 144, 512), BF16),
            pltpu.VMEM((2, 80, 512), BF16),
            pltpu.VMEM((2, 80, 512), BF16),
            pltpu.VMEM((48, 1024), BF16),
            pltpu.VMEM((48, 1024), BF16),
            pltpu.SemaphoreType.DMA((MESSAGES,)),
            pltpu.SemaphoreType.DMA((MESSAGES,)),
        ],
        compiler_params=pltpu.CompilerParams(
            collective_id=0, has_side_effects=True, vmem_limit_bytes=50 * 2**20
        ),
    )(features, kern, cot)
    return (
        resp.reshape(32, 1, 1024),
        fgrad.reshape(2, 32, 4096).transpose(1, 0, 2),
        kgrad.reshape(27, 32, 512).transpose(1, 0, 2),
    )


def solution(mesh):
    in_specs = (P("chan", "depth", None), P("chan", None, None), P("chan", "depth", None))
    out_specs = (P("chan", "depth", None), P("chan", "depth", None), P("chan", None, None))
    return jax.shard_map(
        on_device, mesh=mesh, in_specs=in_specs, out_specs=out_specs, check_vma=False
    )
```

```python
import jax
import jax.numpy as jnp
from jax import lax
from jax.experimental import pallas as pl
from jax.experimental.pallas import tpu as pltpu
from jax.sharding import PartitionSpec as P

BF16 = jnp.bfloat16
F32 = jnp.float32
MESH = pl.DeviceIdType.MESH
SPAN = 250.0
MESSAGES = 136
VMEM_MIB = 40


def near(i):
    return i + 1 - 2 * (i % 2)


def far(i):
    return 3 - i


def ring_order(half):
    return (near, far) if half == 0 else (far, near)


def bound_of(values):
    rows, lanes = values.shape
    top = jnp.max(jnp.abs(values).reshape(rows // 16, 16, lanes), axis=0)
    return jnp.maximum(top, 1e-30).astype(BF16).astype(F32)


def encode(values, bound):
    rows, lanes = values.shape
    blocks = values.reshape(rows // 16, 16, lanes)
    code = jnp.exp2(jnp.abs(blocks) * (SPAN / bound)[None] - SPAN / 2)
    return jnp.where(blocks < 0, -code, code).reshape(rows, lanes).astype(BF16)


def decode(code, bound, scale=1.0):
    rows, lanes = code.shape
    blocks = code.astype(F32).reshape(rows // 16, 16, lanes)
    size = (jnp.log2(jnp.abs(blocks)) + SPAN / 2) * (bound * (scale / SPAN))[None]
    return jnp.where(blocks < 0, -size, size).reshape(rows, lanes)


def dot(a, b, dims):
    return lax.dot_general(a, b, (dims, ((), ())), preferred_element_type=F32)


def kernel(
    feat_in, kern_in, cot, resp, fgrad, codes, run,
    feat, kern, perm, patches, cells_out, cells_in, gathered, terms, spread,
    part, sy1, ry1, sy2, ry2, sz1, rz1, sz2, rz2,
    sc, rc, sx1, rx1, sx2, rx2, sz, rz, local_sem, send_sem, recv_sem,
):
    chan = lax.axis_index("chan")
    depth = lax.axis_index("depth")
    x, zl, core = chan // 4, (chan // 2) % 2, chan % 2
    zh, y = depth // 4, depth % 4
    columns = (x, near(x), far(x), near(far(x)))
    to_core = (chan + 1 - 2 * core, depth)
    to_zl = (4 * x + 2 * (1 - zl) + core, depth)
    up = (chan, (depth + 1) % 16)
    down = (chan, (depth + 15) % 16)

    def opposite(i):
        return near(far(i))

    def to_x(step):
        return (4 * step(x) + 2 * zl + core, depth)

    def to_y(step):
        return (chan, 4 * zh + step(y))

    def to_zh(step):
        return (chan, 4 * step(zh) + y)

    partners = (
        to_core, to_zl, up, down, to_x(opposite),
        to_x(near), to_x(far), to_y(near), to_y(far), to_zh(near), to_zh(far),
    )
    barrier = pltpu.get_barrier_semaphore()
    for partner in partners:
        pl.semaphore_signal(barrier, inc=1, device_id=partner, device_id_type=MESH)
    load_cot = pltpu.make_async_copy(cot, gathered.at[0, x, zl, core], local_sem.at[0])
    load_feat = pltpu.make_async_copy(feat_in, feat, local_sem.at[1])
    load_kern = pltpu.make_async_copy(kern_in, kern, local_sem.at[2])
    load_cot.start()
    load_feat.start()
    load_kern.start()

    lane_in = lax.broadcasted_iota(jnp.int32, (512, 512), 0)
    lane_out = lax.broadcasted_iota(jnp.int32, (512, 512), 1)
    target = (
        ((lane_in >> 6) & 1) * 256 + (lane_in & 1) * 128
        + (lane_in >> 7) * 32 + ((lane_in & 63) >> 1)
    )
    perm[...] = jnp.where(target == lane_out, 1.0, 0.0).astype(BF16)
    pl.semaphore_wait(barrier, len(partners))

    copies = []

    def send(src, dst, device):
        at = len(copies)
        copy = pltpu.make_async_remote_copy(
            src_ref=src, dst_ref=dst, send_sem=send_sem.at[at], recv_sem=recv_sem.at[at],
            device_id=device, device_id_type=MESH,
        )
        copy.start()
        copies.append(copy)
        return copy

    sent = {}
    steps_x = (None, near, far, opposite)

    def cot_start():
        place = gathered.at[0, x, zl, core]
        sent["z"] = send(cot, place, to_zl)
        for k in (1, 2, 3):
            sent["own", k] = send(cot, place, to_x(steps_x[k]))
        sent["core", 0] = send(cot, place, to_core)
        sent["down"] = send(cot, gathered.at[1, x, zl, core], down)

    def cot_z():
        sent["z"].wait_recv()
        place = gathered.at[0, x, 1 - zl, core]
        sent["core", 4] = send(place, place, to_core)
        for k in (1, 2, 3):
            sent["other", k] = send(place, place, to_x(steps_x[k]))

    def cot_core(k):
        sent["own", k].wait_recv()
        sent["other", k].wait_recv()
        place = gathered.at[0, columns[k], :, core]
        sent["core", k] = send(place, place, to_core)

    here = set()

    def cot_wait(k):
        if k in here:
            return
        here.add(k)
        if k == 0:
            load_cot.wait()
            sent["core", 4].wait_recv()
        sent["core", k].wait_recv()

    moves = {}

    def next_z():
        sent["down"].wait_recv()
        place = gathered.at[1, x, zl, core]
        moves["z"] = send(place, place, to_zl)

    def next_x():
        moves["z"].wait_recv()
        pair = gathered.at[1, x, :, core]
        moves["near"] = send(pair, pair, to_x(near))
        moves["far"] = send(pair, pair, to_x(far))
        moves["own_core"] = send(pair, pair, to_core)

    def next_opposite():
        moves["near"].wait_recv()
        first = gathered.at[1, near(x), :, core, 0:16]
        moves["opp0"] = send(first, first, to_x(far))
        block = gathered.at[1, near(x), :, core]
        moves["near_core"] = send(block, block, to_core)
        moves["far"].wait_recv()
        second = gathered.at[1, far(x), :, core, 16:32]
        moves["opp1"] = send(second, second, to_x(near))
        block = gathered.at[1, far(x), :, core]
        moves["far_core"] = send(block, block, to_core)

    def next_last():
        moves["opp0"].wait_recv()
        moves["opp1"].wait_recv()
        block = gathered.at[1, opposite(x), :, core]
        moves["opp_core"] = send(block, block, to_core)

    def next_wait():
        for name in ("own_core", "near_core", "far_core", "opp_core"):
            moves[name].wait_recv()

    def split_cells(plane):
        rows = feat[:, plane, :]
        stacked = jnp.concatenate([rows[:, 512 * k : 512 * k + 512] for k in range(8)], axis=0)
        sorted_cells = dot(stacked, perm[...], ((1,), (0,))).astype(BF16)
        return [
            jnp.concatenate(
                [sorted_cells[32 * k : 32 * k + 32, 128 * q : 128 * q + 128] for k in range(8)],
                axis=1,
            )
            for q in range(4)
        ]

    lane = lax.broadcasted_iota(jnp.int32, (32, 1024), 1)
    not_first_col = jnp.where((lane & 31) > 0, 1.0, 0.0).astype(BF16)
    not_first_row = jnp.where(lane >= 32, 1.0, 0.0).astype(BF16)

    def right(v):
        return pltpu.roll(v, 1, 1) * not_first_col

    def lower(v):
        return pltpu.roll(v, 32, 1) * not_first_row

    def lay_patches(a, cells):
        ee, eo, oe, oo = cells
        eo_r, oo_r = right(eo), right(oo)
        rows = (
            (lower(oo_r), lower(oe), lower(oo)),
            (eo_r, ee, eo),
            (oo_r, oe, oo),
        )
        for b in range(3):
            for c in range(3):
                at = (9 * a + 3 * b + c) * 32
                patches[at : at + 32] = rows[b][c]

    def feat_odd():
        load_feat.wait()
        cells = split_cells(1)
        for q in range(4):
            cells_out[q] = cells[q]
        sent["up"] = send(cells_out, cells_in, up)
        lay_patches(2, cells)

    def feat_even():
        lay_patches(1, split_cells(0))
        patches[864:896] = jnp.zeros((32, 1024), BF16)

    def feat_below():
        sent["up"].wait_recv()
        has_below = jnp.where(depth > 0, 1.0, 0.0).astype(BF16)
        lay_patches(0, [cells_in[q] * has_below for q in range(4)])

    grads = {}

    def grad(k, h):
        first, second = ring_order(h)
        cot_wait(k)
        weights = gathered[0, columns[k]].reshape(128, 1024)
        value = dot(patches[448 * h : 448 * h + 448], weights, ((1,), (1,)))
        for q in range(4):
            part[k, h, q, 0:112] = value[112 * q : 112 * q + 112]
        bound = bound_of(value)
        run[columns[k], h] = bound
        sy1[k, h, 0:112] = encode(part[k, h, first(y), 0:112], bound)
        sy1[k, h, 112:224] = encode(part[k, h, second(first(y)), 0:112], bound)
        sy1[k, h, 224:240] = bound.astype(BF16)
        grads[k, h] = [send(sy1.at[k, h], ry1.at[k, h], to_y(first))]

    def merge_bound(k, h, other):
        bound = jnp.maximum(run[columns[k], h], other)
        run[columns[k], h] = bound
        return bound

    def y2(k, h):
        first, second = ring_order(h)
        grads[k, h][0].wait_recv()
        other = ry1[k, h, 224:240].astype(F32)
        bound = merge_bound(k, h, other)
        part[k, h, second(y), 0:112] += decode(ry1[k, h, 112:224], other)
        sy2[k, h, 0:112] = encode(part[k, h, second(y), 0:112], 2 * bound)
        sy2[k, h, 112:128] = bound.astype(BF16)
        grads[k, h] = [send(sy2.at[k, h], ry2.at[k, h], to_y(second))]
        part[k, h, y, 0:112] += decode(ry1[k, h, 0:112], other)

    def cells_at(i):
        return pl.ds(pl.multiple_of(32 * i, 32), 32)

    def z1(k, h):
        first, second = ring_order(h)
        grads[k, h][0].wait_recv()
        other = ry2[k, h, 112:128].astype(F32)
        bound = merge_bound(k, h, other)
        part[k, h, y, 0:112] += decode(ry2[k, h, 0:112], 2 * other)
        part[k, h, y, 112:128] = jnp.zeros((16, 128), F32)
        sz1[k, h, 0:32] = encode(part[k, h, y, cells_at(first(zh))], 4 * bound)
        sz1[k, h, 32:64] = encode(part[k, h, y, cells_at(second(first(zh)))], 4 * bound)
        sz1[k, h, 64:80] = bound.astype(BF16)
        grads[k, h] = [send(sz1.at[k, h], rz1.at[k, h], to_zh(first))]

    def z2(k, h):
        first, second = ring_order(h)
        grads[k, h][0].wait_recv()
        other = rz1[k, h, 64:80].astype(F32)
        bound = merge_bound(k, h, other)
        part[k, h, y, cells_at(second(zh))] += decode(rz1[k, h, 32:64], 4 * other)
        sz2[k, h, 0:32] = encode(part[k, h, y, cells_at(second(zh))], 8 * bound)
        sz2[k, h, 32:48] = bound.astype(BF16)
        grads[k, h] = [send(sz2.at[k, h], rz2.at[k, h], to_zh(second))]
        part[k, h, y, cells_at(zh)] += decode(rz1[k, h, 0:32], 4 * other)

    def back_z1(k, h):
        first, second = ring_order(h)
        grads[k, h][0].wait_recv()
        other = rz2[k, h, 32:48].astype(F32)
        bound = merge_bound(k, h, other)
        total = part[k, h, y, cells_at(zh)] + decode(rz2[k, h, 0:32], 8 * other)
        codes[columns[k], h, y, cells_at(zh)] = encode(total, 16 * bound)
        own = codes.at[columns[k], h, y, cells_at(zh)]
        grads[k, h] = [send(own, own, to_zh(second)), send(own, own, to_zh(first))]

    def back_z2(k, h):
        first, second = ring_order(h)
        grads[k, h][0].wait_recv()
        block = codes.at[columns[k], h, y, cells_at(second(zh))]
        grads[k, h][0] = send(block, block, to_zh(first))

    def back_y1(k, h):
        first, second = ring_order(h)
        grads[k, h][0].wait_recv()
        grads[k, h][1].wait_recv()
        block = codes.at[columns[k], h, y, 0:112]
        grads[k, h] = [send(block, block, to_y(second)), send(block, block, to_y(first))]

    def back_y2(k, h):
        first, second = ring_order(h)
        grads[k, h][0].wait_recv()
        block = codes.at[columns[k], h, second(y), 0:112]
        grads[k, h][0] = send(block, block, to_y(first))

    def back_wait(k, h):
        grads[k, h][0].wait_recv()
        grads[k, h][1].wait_recv()

    sums = {}

    def resp_terms(i):
        if i == 0:
            load_kern.wait()
        value = dot(kern[:, 128 * i : 128 * i + 128], patches[0:864], ((0,), (0,)))
        terms[i] = value.reshape(2, 2, 32, 1024)

    def resp_core():
        bound = bound_of(terms[:, :, 1 - core].reshape(256, 1024))
        for i in range(4):
            for j in range(2):
                at = 64 * i + 32 * j
                sc[at : at + 32] = encode(terms[i, j, 1 - core], bound)
        sc[256:272] = bound.astype(BF16)
        sums["core"] = send(sc, rc, to_core)

    def resp_x1():
        sums["core"].wait_recv()
        other = rc[256:272].astype(F32)
        for i in range(4):
            for j in range(2):
                at = 64 * i + 32 * j
                terms[i, j, core] += decode(rc[at : at + 32], other)
        for h in range(2):
            first, second = ring_order(h)
            lanes = slice(512 * h, 512 * h + 512)
            blocks = [
                terms[i, j, core, :, lanes] for i in (first(x), second(first(x))) for j in range(2)
            ]
            value = jnp.concatenate(blocks, axis=0)
            bound = bound_of(value)
            sx1[h, 0:128] = encode(value, bound)
            sx1[h, 128:144] = bound.astype(BF16)
            sums["x1", h] = send(sx1.at[h], rx1.at[h], to_x(first))

    def resp_x2():
        for h in range(2):
            first, second = ring_order(h)
            lanes = slice(512 * h, 512 * h + 512)
            sums["x1", h].wait_recv()
            other = rx1[h, 128:144].astype(F32)
            for n, i in enumerate((x, second(x))):
                for j in range(2):
                    at = 64 * n + 32 * j
                    terms[i, j, core, :, lanes] += decode(rx1[h, at : at + 32], other)
            value = jnp.concatenate(
                [terms[second(x), j, core, :, lanes] for j in range(2)], axis=0
            )
            bound = bound_of(value)
            sx2[h, 0:64] = encode(value, bound)
            sx2[h, 64:80] = bound.astype(BF16)
            sums["x2", h] = send(sx2.at[h], rx2.at[h], to_x(second))

    def resp_z():
        for h in range(2):
            lanes = slice(512 * h, 512 * h + 512)
            sums["x2", h].wait_recv()
            other = rx2[h, 64:80].astype(F32)
            for j in range(2):
                terms[x, j, core, :, lanes] += decode(rx2[h, 32 * j : 32 * j + 32], other)
        value = terms[x, 1 - zl, core]
        bound = bound_of(value)
        sz[0:32] = encode(value, bound)
        sz[32:48] = bound.astype(BF16)
        sums["z"] = send(sz, rz, to_zl)

    def resp_result():
        sums["z"].wait_recv()
        total = terms[x, zl, core] + decode(rz[0:32], rz[32:48].astype(F32))
        resp[...] = total.astype(BF16)

    not_last_col = jnp.where((lane & 31) < 31, 1.0, 0.0)
    not_last_row = jnp.where(lane < 992, 1.0, 0.0)

    def left(v):
        return pltpu.roll(v, 1023, 1) * not_last_col

    def upper(v):
        return pltpu.roll(v, 992, 1) * not_last_row

    def join_cells(plane):
        def tap(b, c):
            at = (3 * b + c) * 32
            return spread[at : at + 32]

        cells = [
            tap(1, 1),
            tap(1, 2) + left(tap(1, 0)),
            tap(2, 1) + upper(tap(0, 1)),
            tap(2, 2) + left(tap(2, 0)) + upper(tap(0, 2) + left(tap(0, 0))),
        ]
        cells = [v.astype(BF16) for v in cells]
        stacked = jnp.concatenate(
            [
                jnp.concatenate([v[:, 128 * k : 128 * k + 128] for v in cells], axis=1)
                for k in range(8)
            ],
            axis=0,
        )
        rows = dot(stacked, perm[...], ((1,), (1,))).astype(BF16)
        for k in range(8):
            fgrad[32 * plane : 32 * plane + 32, 512 * k : 512 * k + 512] = rows[
                32 * k : 32 * k + 32
            ]

    def feature_even():
        for k in range(4):
            cot_wait(k)
        cots = gathered[0].reshape(512, 1024)
        spread[...] = dot(kern[288:576], cots, ((1,), (0,)))
        join_cells(0)

    def feature_odd():
        next_wait()
        has_above = jnp.where(depth < 15, 1.0, 0.0)
        spread[...] = dot(kern[0:288], gathered[1].reshape(512, 1024), ((1,), (0,))) * has_above
        spread[...] += dot(kern[576:864], gathered[0].reshape(512, 1024), ((1,), (0,)))
        join_cells(1)

    cot_start()
    feat_odd()
    feat_even()
    cot_z()
    next_z()
    grad(0, 1)
    feat_below()
    grad(0, 0)
    cot_core(2)
    cot_core(1)
    resp_terms(0)
    resp_terms(1)
    resp_terms(2)
    resp_terms(3)
    grad(2, 1)
    grad(1, 1)
    cot_core(3)
    grad(1, 0)
    grad(2, 0)
    y2(0, 0)
    y2(0, 1)
    resp_core()
    grad(3, 0)
    grad(3, 1)
    y2(2, 1)
    next_x()
    feature_even()
    y2(1, 0)
    y2(1, 1)
    resp_x1()
    y2(2, 0)
    z1(0, 0)
    z1(0, 1)
    y2(3, 1)
    z1(1, 0)
    y2(3, 0)
    next_opposite()
    z1(2, 0)
    z1(2, 1)
    z2(0, 0)
    z1(1, 1)
    z2(0, 1)
    z1(3, 1)
    z1(3, 0)
    z2(1, 0)
    resp_x2()
    z2(2, 1)
    z2(2, 0)
    back_z1(0, 0)
    back_z1(0, 1)
    next_last()
    z2(1, 1)
    z2(3, 0)
    z2(3, 1)
    back_z1(2, 1)
    feature_odd()
    back_z1(1, 0)
    back_z1(1, 1)
    back_z1(2, 0)
    back_z2(0, 0)
    back_z2(0, 1)
    resp_z()
    back_z1(3, 1)
    back_z1(3, 0)
    back_z2(2, 1)
    back_z2(1, 0)
    back_z2(1, 1)
    back_z2(2, 0)
    back_y1(0, 1)
    back_y1(0, 0)
    back_z2(3, 1)
    back_z2(3, 0)
    resp_result()
    back_y1(2, 1)
    back_y1(1, 0)
    back_y1(1, 1)
    back_y1(2, 0)
    back_y2(0, 1)
    back_y1(3, 1)
    back_y2(0, 0)
    back_y1(3, 0)
    back_y2(2, 1)
    back_y2(1, 0)
    back_y2(1, 1)
    back_y2(2, 0)
    back_y2(3, 1)
    back_y2(3, 0)
    back_wait(0, 1)
    back_wait(0, 0)
    back_wait(1, 1)
    back_wait(1, 0)
    back_wait(2, 1)
    back_wait(2, 0)
    back_wait(3, 1)
    back_wait(3, 0)
    for copy in copies:
        copy.wait_send()


def finish(fg_in, resp_in, codes, run, fgrad, resp, kgrad, fg_v, kg_v, sem):
    copy_resp = pltpu.make_async_copy(resp_in, resp, sem.at[8])
    copy_resp.start()
    for plane in range(2):
        fg_v[:, plane, :] = fg_in[32 * plane : 32 * plane + 32]
    copy_fg = pltpu.make_async_copy(fg_v, fgrad, sem.at[9])
    copy_fg.start()
    copies = [copy_resp, copy_fg]
    for h in range(2):
        for q in range(4):
            at = 448 * h + 112 * q
            count = min(112, 864 - at)
            rows = pl.ds(at, count)
            for xb in range(4):
                kg_v[rows, 128 * xb : 128 * xb + 128] = decode(
                    codes[xb, h, q, 0:count], 16 * run[xb, h], 1.0 / 128
                )
            copy = pltpu.make_async_copy(kg_v.at[rows], kgrad.at[rows], sem.at[4 * h + q])
            copy.start()
            copies.append(copy)
    for copy in copies:
        copy.wait()


def on_device(features, kernel_block, cotangent):
    kern = kernel_block.transpose(1, 0, 2).reshape(864, 512)
    cot = cotangent.reshape(32, 1024)
    shape = jax.ShapeDtypeStruct
    vmem = pl.BlockSpec(memory_space=pltpu.VMEM)
    hbm = pl.BlockSpec(memory_space=pltpu.HBM)
    resp, fgrad, codes, run = pl.pallas_call(
        kernel,
        out_shape=(
            shape((32, 1024), BF16), shape((64, 4096), BF16),
            shape((4, 2, 4, 128, 128), BF16), shape((4, 2, 16, 128), F32),
        ),
        in_specs=[hbm] * 3,
        out_specs=(vmem,) * 4,
        scratch_shapes=[
            pltpu.VMEM((32, 2, 4096), BF16),
            pltpu.VMEM((864, 512), BF16),
            pltpu.VMEM((512, 512), BF16),
            pltpu.VMEM((896, 1024), BF16),
            pltpu.VMEM((4, 32, 1024), BF16),
            pltpu.VMEM((4, 32, 1024), BF16),
            pltpu.VMEM((2, 4, 2, 2, 32, 1024), BF16),
            pltpu.VMEM((4, 2, 2, 32, 1024), F32),
            pltpu.VMEM((288, 1024), F32),
            pltpu.VMEM((4, 2, 4, 128, 128), F32),
        ]
        + [
            pltpu.VMEM((4, 2, rows, 128), BF16)
            for rows in (240, 240, 128, 128, 80, 80, 48, 48)
        ]
        + [
            pltpu.VMEM((272, 1024), BF16),
            pltpu.VMEM((272, 1024), BF16),
            pltpu.VMEM((2, 144, 512), BF16),
            pltpu.VMEM((2, 144, 512), BF16),
            pltpu.VMEM((2, 80, 512), BF16),
            pltpu.VMEM((2, 80, 512), BF16),
            pltpu.VMEM((48, 1024), BF16),
            pltpu.VMEM((48, 1024), BF16),
            pltpu.SemaphoreType.DMA((3,)),
            pltpu.SemaphoreType.DMA((MESSAGES,)),
            pltpu.SemaphoreType.DMA((MESSAGES,)),
        ],
        compiler_params=pltpu.CompilerParams(
            collective_id=0, has_side_effects=True, vmem_limit_bytes=VMEM_MIB * 2**20
        ),
    )(features, kern, cot)
    fgrad, resp, kgrad = pl.pallas_call(
        finish,
        out_shape=(shape((32, 2, 4096), BF16), shape((32, 1024), BF16), shape((864, 512), F32)),
        in_specs=[vmem] * 4,
        out_specs=(hbm,) * 3,
        scratch_shapes=[
            pltpu.VMEM((32, 2, 4096), BF16),
            pltpu.VMEM((864, 512), F32),
            pltpu.SemaphoreType.DMA((10,)),
        ],
        compiler_params=pltpu.CompilerParams(vmem_limit_bytes=16 * 2**20),
    )(fgrad, resp, codes, run)
    return (
        resp.reshape(32, 1, 1024), fgrad, kgrad.reshape(27, 32, 512).transpose(1, 0, 2),
    )


def solution(mesh):
    in_specs = (P("chan", "depth", None), P("chan", None, None), P("chan", "depth", None))
    out_specs = (P("chan", "depth", None), P("chan", "depth", None), P("chan", None, None))
    return jax.shard_map(
        on_device, mesh=mesh, in_specs=in_specs, out_specs=out_specs, check_vma=False
    )
```

```python
import jax
import jax.numpy as jnp
from jax import lax
from jax.experimental import pallas as pl
from jax.experimental.pallas import tpu as pltpu
from jax.sharding import PartitionSpec as P

BF16 = jnp.bfloat16
F32 = jnp.float32
MESH = pl.DeviceIdType.MESH
SPAN = 250.0
MESSAGES = 136
VMEM_MIB = 56


def near(i):
    return i + 1 - 2 * (i % 2)


def far(i):
    return 3 - i


def ring_order(half):
    return (near, far) if half == 0 else (far, near)


def bound_of(values):
    rows, lanes = values.shape
    top = jnp.max(jnp.abs(values).reshape(rows // 16, 16, lanes), axis=0)
    return jnp.maximum(top, 1e-30).astype(BF16).astype(F32)


def encode(values, bound):
    rows, lanes = values.shape
    blocks = values.reshape(rows // 16, 16, lanes)
    code = jnp.exp2(jnp.abs(blocks) * (SPAN / bound)[None] - SPAN / 2)
    return jnp.where(blocks < 0, -code, code).reshape(rows, lanes).astype(BF16)


def decode(code, bound, scale=1.0):
    rows, lanes = code.shape
    blocks = code.astype(F32).reshape(rows // 16, 16, lanes)
    size = (jnp.log2(jnp.abs(blocks)) + SPAN / 2) * (bound * (scale / SPAN))[None]
    return jnp.where(blocks < 0, -size, size).reshape(rows, lanes)


def dot(a, b, dims):
    return lax.dot_general(a, b, (dims, ((), ())), preferred_element_type=F32)


def kernel(
    feat_in, kern_in, cot, resp_out, fgrad_out, codes_out, run_out,
    resp, fgrad, codes, run, feat, kern, perm, patches, gathered, terms, spread,
    part, sy1, ry1, sy2, ry2, sz1, rz1, sz2, rz2,
    sc, rc, sx1, rx1, sx2, rx2, sz, rz, su, ru, local_sem, send_sem, recv_sem,
):
    chan = lax.axis_index("chan")
    depth = lax.axis_index("depth")
    x, zl, core = chan // 4, (chan // 2) % 2, chan % 2
    zh, y = depth // 4, depth % 4
    columns = (x, near(x), far(x), near(far(x)))
    to_core = (chan + 1 - 2 * core, depth)
    to_zl = (4 * x + 2 * (1 - zl) + core, depth)
    up = (chan, (depth + 1) % 16)
    down = (chan, (depth + 15) % 16)

    def opposite(i):
        return near(far(i))

    def to_x(step):
        return (4 * step(x) + 2 * zl + core, depth)

    def to_y(step):
        return (chan, 4 * zh + step(y))

    def to_zh(step):
        return (chan, 4 * step(zh) + y)

    partners = (
        to_core, to_zl, up, down, to_x(opposite),
        to_x(near), to_x(far), to_y(near), to_y(far), to_zh(near), to_zh(far),
    )
    barrier = pltpu.get_barrier_semaphore()
    for partner in partners:
        pl.semaphore_signal(barrier, inc=1, device_id=partner, device_id_type=MESH)
    load_cot = pltpu.make_async_copy(cot, gathered.at[0, x, zl, core], local_sem.at[0])
    load_feat = pltpu.make_async_copy(feat_in, feat, local_sem.at[1])
    load_kern = pltpu.make_async_copy(kern_in, kern, local_sem.at[2])
    load_cot.start()
    load_feat.start()
    load_kern.start()

    lane_in = lax.broadcasted_iota(jnp.int32, (512, 512), 0)
    lane_out = lax.broadcasted_iota(jnp.int32, (512, 512), 1)
    target = (
        ((lane_in >> 6) & 1) * 256 + (lane_in & 1) * 128
        + (lane_in >> 7) * 32 + ((lane_in & 63) >> 1)
    )
    perm[...] = jnp.where(target == lane_out, 1.0, 0.0).astype(BF16)
    pl.semaphore_wait(barrier, len(partners))

    copies = []

    def send(src, dst, device):
        at = len(copies)
        copy = pltpu.make_async_remote_copy(
            src_ref=src, dst_ref=dst, send_sem=send_sem.at[at], recv_sem=recv_sem.at[at],
            device_id=device, device_id_type=MESH,
        )
        copy.start()
        copies.append(copy)
        return copy

    sent = {}
    steps_x = (None, near, far, opposite)

    def cot_start(j):
        place = gathered.at[j, x, zl, core]
        source = place if j else cot
        if j:
            sent["down"].wait_recv()
        sent[j, "z"] = send(source, place, to_zl)
        if not j:
            sent["down"] = send(cot, gathered.at[1, x, zl, core], down)
        for k in (1, 2, 3):
            sent[j, "own", k] = send(source, place, to_x(steps_x[k]))
        sent[j, "core", 0] = send(source, place, to_core)

    def cot_z(j):
        sent[j, "z"].wait_recv()
        place = gathered.at[j, x, 1 - zl, core]
        sent[j, "core", 4] = send(place, place, to_core)
        for k in (1, 2, 3):
            sent[j, "other", k] = send(place, place, to_x(steps_x[k]))

    def cot_core(j, k):
        sent[j, "own", k].wait_recv()
        sent[j, "other", k].wait_recv()
        place = gathered.at[j, columns[k], :, core]
        sent[j, "core", k] = send(place, place, to_core)

    here = set()

    def cot_wait(j, k):
        if (j, k) in here:
            return
        here.add((j, k))
        if k == 0:
            if j == 0:
                load_cot.wait()
            sent[j, "core", 4].wait_recv()
        sent[j, "core", k].wait_recv()

    def split_cells(plane):
        rows = feat[:, plane, :]
        stacked = jnp.concatenate([rows[:, 512 * k : 512 * k + 512] for k in range(8)], axis=0)
        sorted_cells = dot(stacked, perm[...], ((1,), (0,))).astype(BF16)
        return [
            jnp.concatenate(
                [sorted_cells[32 * k : 32 * k + 32, 128 * q : 128 * q + 128] for k in range(8)],
                axis=1,
            )
            for q in range(4)
        ]

    lane = lax.broadcasted_iota(jnp.int32, (32, 1024), 1)
    not_first_col = jnp.where((lane & 31) > 0, 1.0, 0.0).astype(BF16)
    not_first_row = jnp.where(lane >= 32, 1.0, 0.0).astype(BF16)

    def right(v):
        return pltpu.roll(v, 1, 1) * not_first_col

    def lower(v):
        return pltpu.roll(v, 32, 1) * not_first_row

    def lay_patches(a, cells):
        ee, eo, oe, oo = cells
        eo_r, oo_r = right(eo), right(oo)
        rows = (
            (lower(oo_r), lower(oe), lower(oo)),
            (eo_r, ee, eo),
            (oo_r, oe, oo),
        )
        for b in range(3):
            for c in range(3):
                at = (9 * a + 3 * b + c) * 32
                patches[at : at + 32] = rows[b][c]

    def feat_odd():
        load_feat.wait()
        cells = split_cells(1)
        lay_patches(2, cells)

    def feat_even():
        lay_patches(1, split_cells(0))
        patches[864:896] = jnp.zeros((32, 1024), BF16)

    has_above = jnp.where(depth < 15, 1.0, 0.0)
    has_below = jnp.where(depth > 0, 1.0, 0.0)

    grads = {}

    def grad(k, h):
        first, second = ring_order(h)
        cot_wait(0, k)
        weights = gathered[0, columns[k]].reshape(128, 1024)
        if h:
            value = dot(patches[448:896], weights, ((1,), (1,)))
        else:
            cot_wait(1, k)
            above = gathered[1, columns[k]].reshape(128, 1024)
            value = jnp.concatenate(
                [
                    dot(patches[576:864], above, ((1,), (1,))) * has_above,
                    dot(patches[288:448], weights, ((1,), (1,))),
                ],
                axis=0,
            )
        for q in range(4):
            part[k, h, q, 0:112] = value[112 * q : 112 * q + 112]
        bound = bound_of(value)
        run[columns[k], h] = bound
        sy1[k, h, 0:112] = encode(part[k, h, first(y), 0:112], bound)
        sy1[k, h, 112:224] = encode(part[k, h, second(first(y)), 0:112], bound)
        sy1[k, h, 224:240] = bound.astype(BF16)
        grads[k, h] = [send(sy1.at[k, h], ry1.at[k, h], to_y(first))]

    def merge_bound(k, h, other):
        bound = jnp.maximum(run[columns[k], h], other)
        run[columns[k], h] = bound
        return bound

    def y2(k, h):
        first, second = ring_order(h)
        grads[k, h][0].wait_recv()
        other = ry1[k, h, 224:240].astype(F32)
        bound = merge_bound(k, h, other)
        part[k, h, second(y), 0:112] += decode(ry1[k, h, 112:224], other)
        sy2[k, h, 0:112] = encode(part[k, h, second(y), 0:112], 2 * bound)
        sy2[k, h, 112:128] = bound.astype(BF16)
        grads[k, h] = [send(sy2.at[k, h], ry2.at[k, h], to_y(second))]
        part[k, h, y, 0:112] += decode(ry1[k, h, 0:112], other)

    def cells_at(i):
        return pl.ds(pl.multiple_of(32 * i, 32), 32)

    def z1(k, h):
        first, second = ring_order(h)
        grads[k, h][0].wait_recv()
        other = ry2[k, h, 112:128].astype(F32)
        bound = merge_bound(k, h, other)
        part[k, h, y, 0:112] += decode(ry2[k, h, 0:112], 2 * other)
        part[k, h, y, 112:128] = jnp.zeros((16, 128), F32)
        sz1[k, h, 0:32] = encode(part[k, h, y, cells_at(first(zh))], 4 * bound)
        sz1[k, h, 32:64] = encode(part[k, h, y, cells_at(second(first(zh)))], 4 * bound)
        sz1[k, h, 64:80] = bound.astype(BF16)
        grads[k, h] = [send(sz1.at[k, h], rz1.at[k, h], to_zh(first))]

    def z2(k, h):
        first, second = ring_order(h)
        grads[k, h][0].wait_recv()
        other = rz1[k, h, 64:80].astype(F32)
        bound = merge_bound(k, h, other)
        part[k, h, y, cells_at(second(zh))] += decode(rz1[k, h, 32:64], 4 * other)
        sz2[k, h, 0:32] = encode(part[k, h, y, cells_at(second(zh))], 8 * bound)
        sz2[k, h, 32:48] = bound.astype(BF16)
        grads[k, h] = [send(sz2.at[k, h], rz2.at[k, h], to_zh(second))]
        part[k, h, y, cells_at(zh)] += decode(rz1[k, h, 0:32], 4 * other)

    def back_z1(k, h):
        first, second = ring_order(h)
        grads[k, h][0].wait_recv()
        other = rz2[k, h, 32:48].astype(F32)
        bound = merge_bound(k, h, other)
        total = part[k, h, y, cells_at(zh)] + decode(rz2[k, h, 0:32], 8 * other)
        codes[columns[k], h, y, cells_at(zh)] = encode(total, 16 * bound)
        own = codes.at[columns[k], h, y, cells_at(zh)]
        grads[k, h] = [send(own, own, to_zh(second)), send(own, own, to_zh(first))]

    def back_z2(k, h):
        first, second = ring_order(h)
        grads[k, h][0].wait_recv()
        block = codes.at[columns[k], h, y, cells_at(second(zh))]
        grads[k, h][0] = send(block, block, to_zh(first))

    def back_y1(k, h):
        first, second = ring_order(h)
        grads[k, h][0].wait_recv()
        grads[k, h][1].wait_recv()
        block = codes.at[columns[k], h, y, 0:112]
        grads[k, h] = [send(block, block, to_y(second)), send(block, block, to_y(first))]

    def back_y2(k, h):
        first, second = ring_order(h)
        grads[k, h][0].wait_recv()
        block = codes.at[columns[k], h, second(y), 0:112]
        grads[k, h][0] = send(block, block, to_y(first))

    def back_wait(k, h):
        grads[k, h][0].wait_recv()
        grads[k, h][1].wait_recv()
        keep(codes.at[columns[k], h], codes_out.at[columns[k], h])

    kept = []

    def keep(src, dst):
        copy = pltpu.make_async_copy(src, dst, local_sem.at[3 + len(kept)])
        copy.start()
        kept.append(copy)


    sums = {}

    def resp_terms(p, i):
        if p == 1 and i == 0:
            load_kern.wait()
        taps = slice(0, 288) if p else slice(288, 864)
        rows = patches[576:864] if p else patches[288:864]
        value = dot(kern[taps, 128 * i : 128 * i + 128], rows, ((0,), (0,)))
        terms[p, i] = value.reshape(2, 2, 32, 1024)

    def resp_core(p):
        bound = bound_of(terms[p, :, :, 1 - core].reshape(256, 1024))
        for i in range(4):
            for j in range(2):
                at = 64 * i + 32 * j
                sc[p, at : at + 32] = encode(terms[p, i, j, 1 - core], bound)
        sc[p, 256:272] = bound.astype(BF16)
        sums[p, 2] = send(sc.at[p], rc.at[p], to_core)

    def resp_x1(p):
        sums[p, 2].wait_recv()
        other = rc[p, 256:272].astype(F32)
        for i in range(4):
            for j in range(2):
                at = 64 * i + 32 * j
                terms[p, i, j, core] += decode(rc[p, at : at + 32], other)
        for h in range(2):
            first, second = ring_order(h)
            lanes = slice(512 * h, 512 * h + 512)
            blocks = [
                terms[p, i, j, core, :, lanes]
                for i in (first(x), second(first(x)))
                for j in range(2)
            ]
            value = jnp.concatenate(blocks, axis=0)
            bound = bound_of(value)
            sx1[p, h, 0:128] = encode(value, bound)
            sx1[p, h, 128:144] = bound.astype(BF16)
            sums[p, h] = send(sx1.at[p, h], rx1.at[p, h], to_x(first))

    def resp_x2(p):
        for h in range(2):
            first, second = ring_order(h)
            lanes = slice(512 * h, 512 * h + 512)
            sums[p, h].wait_recv()
            other = rx1[p, h, 128:144].astype(F32)
            for n, i in enumerate((x, second(x))):
                for j in range(2):
                    at = 64 * n + 32 * j
                    terms[p, i, j, core, :, lanes] += decode(rx1[p, h, at : at + 32], other)
            value = jnp.concatenate(
                [terms[p, second(x), j, core, :, lanes] for j in range(2)], axis=0
            )
            bound = bound_of(value)
            sx2[p, h, 0:64] = encode(value, bound)
            sx2[p, h, 64:80] = bound.astype(BF16)
            sums[p, h] = send(sx2.at[p, h], rx2.at[p, h], to_x(second))

    def resp_z(p):
        for h in range(2):
            lanes = slice(512 * h, 512 * h + 512)
            sums[p, h].wait_recv()
            other = rx2[p, h, 64:80].astype(F32)
            for j in range(2):
                terms[p, x, j, core, :, lanes] += decode(
                    rx2[p, h, 32 * j : 32 * j + 32], other
                )
        value = terms[p, x, 1 - zl, core]
        bound = bound_of(value)
        sz[p, 0:32] = encode(value, bound)
        sz[p, 32:48] = bound.astype(BF16)
        sums[p, 2] = send(sz.at[p], rz.at[p], to_zl)

    def resp_sum(p):
        sums[p, 2].wait_recv()
        return terms[p, x, zl, core] + decode(rz[p, 0:32], rz[p, 32:48].astype(F32))

    def resp_up():
        value = resp_sum(1)
        bound = bound_of(value)
        su[0:32] = encode(value, bound)
        su[32:48] = bound.astype(BF16)
        sums["up"] = send(su, ru, up)

    def resp_result():
        total = resp_sum(0)
        sums["up"].wait_recv()
        total += decode(ru[0:32], ru[32:48].astype(F32)) * has_below
        resp[...] = total.astype(BF16)
        keep(resp, resp_out)

    not_last_col = jnp.where((lane & 31) < 31, 1.0, 0.0)
    not_last_row = jnp.where(lane < 992, 1.0, 0.0)

    def left(v):
        return pltpu.roll(v, 1023, 1) * not_last_col

    def upper(v):
        return pltpu.roll(v, 992, 1) * not_last_row

    def join_cells(plane):
        def tap(b, c):
            at = (3 * b + c) * 32
            return spread[at : at + 32]

        cells = [
            tap(1, 1),
            tap(1, 2) + left(tap(1, 0)),
            tap(2, 1) + upper(tap(0, 1)),
            tap(2, 2) + left(tap(2, 0)) + upper(tap(0, 2) + left(tap(0, 0))),
        ]
        cells = [v.astype(BF16) for v in cells]
        stacked = jnp.concatenate(
            [
                jnp.concatenate([v[:, 128 * k : 128 * k + 128] for v in cells], axis=1)
                for k in range(8)
            ],
            axis=0,
        )
        rows = dot(stacked, perm[...], ((1,), (1,))).astype(BF16)
        for k in range(8):
            fgrad[32 * plane : 32 * plane + 32, 512 * k : 512 * k + 512] = rows[
                32 * k : 32 * k + 32
            ]

    def feature_even():
        for k in range(4):
            cot_wait(0, k)
        cots = gathered[0].reshape(512, 1024)
        spread[...] = dot(kern[288:576], cots, ((1,), (0,)))
        join_cells(0)
        keep(fgrad.at[0:32], fgrad_out.at[0:32])

    def feature_odd():
        for k in range(4):
            cot_wait(1, k)
        spread[...] = dot(kern[0:288], gathered[1].reshape(512, 1024), ((1,), (0,))) * has_above
        spread[...] += dot(kern[576:864], gathered[0].reshape(512, 1024), ((1,), (0,)))
        join_cells(1)
        keep(fgrad.at[32:64], fgrad_out.at[32:64])

    cot_start(0)
    feat_odd()
    feat_even()
    resp_terms(1, 0)
    resp_terms(1, 1)
    resp_terms(1, 2)
    resp_terms(1, 3)
    resp_core(1)
    cot_z(0)
    resp_terms(0, 0)
    resp_terms(0, 1)
    resp_terms(0, 2)
    resp_terms(0, 3)
    cot_start(1)
    resp_core(0)
    resp_x1(1)
    cot_core(0, 2)
    cot_core(0, 1)
    grad(0, 1)
    cot_z(1)
    resp_x1(0)
    cot_core(0, 3)
    grad(2, 1)
    grad(1, 1)
    grad(0, 0)
    y2(0, 1)
    grad(3, 1)
    feature_even()
    y2(2, 1)
    y2(0, 0)
    y2(1, 1)
    z1(0, 1)
    resp_x2(1)
    z1(2, 1)
    y2(3, 1)
    z1(0, 0)
    cot_core(1, 2)
    cot_core(1, 1)
    z1(1, 1)
    z2(0, 1)
    grad(2, 0)
    z1(3, 1)
    grad(1, 0)
    cot_core(1, 3)
    z2(2, 1)
    z2(0, 0)
    z2(1, 1)
    back_z1(0, 1)
    grad(3, 0)
    feature_odd()
    y2(2, 0)
    z2(3, 1)
    back_z1(2, 1)
    y2(1, 0)
    back_z1(0, 0)
    back_z1(1, 1)
    resp_x2(0)
    resp_z(1)
    back_z2(0, 1)
    y2(3, 0)
    z1(2, 0)
    back_z1(3, 1)
    back_z2(0, 0)
    z1(1, 0)
    back_z2(2, 1)
    back_y1(0, 1)
    back_z2(1, 1)
    z1(3, 0)
    resp_z(0)
    resp_up()
    z2(2, 0)
    back_y1(2, 1)
    back_z2(3, 1)
    back_y2(0, 1)
    back_y1(0, 0)
    back_y1(1, 1)
    z2(1, 0)
    back_y2(2, 1)
    back_z1(2, 0)
    z2(3, 0)
    back_y1(3, 1)
    back_y2(0, 0)
    back_y2(1, 1)
    back_z1(1, 0)
    back_z2(2, 0)
    back_y2(3, 1)
    back_z1(3, 0)
    resp_result()
    back_z2(1, 0)
    back_y1(2, 0)
    back_z2(3, 0)
    back_y1(1, 0)
    back_y2(2, 0)
    back_y1(3, 0)
    back_y2(1, 0)
    back_y2(3, 0)
    back_wait(0, 1)
    back_wait(0, 0)
    back_wait(1, 1)
    back_wait(1, 0)
    back_wait(2, 1)
    back_wait(2, 0)
    back_wait(3, 1)
    back_wait(3, 0)
    keep(run, run_out)
    for copy in copies:
        copy.wait_send()
    for copy in kept:
        copy.wait()


def finish(fg_in, resp_in, codes_in, run_in, fgrad, resp, kgrad, fg2, codes, run, fg_v, kg_v, sem):
    loads = [
        pltpu.make_async_copy(run_in, run, sem.at[10]),
        pltpu.make_async_copy(fg_in, fg2, sem.at[11]),
        pltpu.make_async_copy(codes_in.at[:, 0], codes.at[0], sem.at[12]),
        pltpu.make_async_copy(codes_in.at[:, 1], codes.at[1], sem.at[13]),
    ]
    for copy in loads:
        copy.start()
    copy_resp = pltpu.make_async_copy(resp_in, resp, sem.at[8])
    copy_resp.start()
    loads[0].wait()
    loads[1].wait()
    for plane in range(2):
        fg_v[:, plane, :] = fg2[32 * plane : 32 * plane + 32]
    copy_fg = pltpu.make_async_copy(fg_v, fgrad, sem.at[9])
    copy_fg.start()
    copies = [copy_resp, copy_fg]
    for h in range(2):
        loads[2 + h].wait()
        for q in range(4):
            at = 448 * h + 112 * q
            count = min(112, 864 - at)
            rows = pl.ds(at, count)
            for xb in range(4):
                kg_v[rows, 128 * xb : 128 * xb + 128] = decode(
                    codes[h, xb, q, 0:count], 16 * run[xb, h], 1.0 / 128
                )
            copy = pltpu.make_async_copy(kg_v.at[rows], kgrad.at[rows], sem.at[4 * h + q])
            copy.start()
            copies.append(copy)
    for copy in copies:
        copy.wait()


def on_device(features, kernel_block, cotangent):
    kern = kernel_block.transpose(1, 0, 2).reshape(864, 512)
    cot = cotangent.reshape(32, 1024)
    shape = jax.ShapeDtypeStruct
    hbm = pl.BlockSpec(memory_space=pltpu.HBM)
    resp, fgrad, codes, run = pl.pallas_call(
        kernel,
        out_shape=(
            shape((32, 1024), BF16), shape((64, 4096), BF16),
            shape((4, 2, 4, 128, 128), BF16), shape((4, 2, 16, 128), F32),
        ),
        in_specs=[hbm] * 3,
        out_specs=(hbm,) * 4,
        scratch_shapes=[
            pltpu.VMEM((32, 1024), BF16),
            pltpu.VMEM((64, 4096), BF16),
            pltpu.VMEM((4, 2, 4, 128, 128), BF16),
            pltpu.VMEM((4, 2, 16, 128), F32),
            pltpu.VMEM((32, 2, 4096), BF16),
            pltpu.VMEM((864, 512), BF16),
            pltpu.VMEM((512, 512), BF16),
            pltpu.VMEM((896, 1024), BF16),
            pltpu.VMEM((2, 4, 2, 2, 32, 1024), BF16),
            pltpu.VMEM((2, 4, 2, 2, 32, 1024), F32),
            pltpu.VMEM((288, 1024), F32),
            pltpu.VMEM((4, 2, 4, 128, 128), F32),
        ]
        + [
            pltpu.VMEM((4, 2, rows, 128), BF16)
            for rows in (240, 240, 128, 128, 80, 80, 48, 48)
        ]
        + [
            pltpu.VMEM((2, 272, 1024), BF16),
            pltpu.VMEM((2, 272, 1024), BF16),
            pltpu.VMEM((2, 2, 144, 512), BF16),
            pltpu.VMEM((2, 2, 144, 512), BF16),
            pltpu.VMEM((2, 2, 80, 512), BF16),
            pltpu.VMEM((2, 2, 80, 512), BF16),
            pltpu.VMEM((2, 48, 1024), BF16),
            pltpu.VMEM((2, 48, 1024), BF16),
            pltpu.VMEM((48, 1024), BF16),
            pltpu.VMEM((48, 1024), BF16),
            pltpu.SemaphoreType.DMA((16,)),
            pltpu.SemaphoreType.DMA((MESSAGES,)),
            pltpu.SemaphoreType.DMA((MESSAGES,)),
        ],
        compiler_params=pltpu.CompilerParams(
            collective_id=0, has_side_effects=True, vmem_limit_bytes=VMEM_MIB * 2**20
        ),
    )(features, kern, cot)
    fgrad, resp, kgrad = pl.pallas_call(
        finish,
        out_shape=(shape((32, 2, 4096), BF16), shape((32, 1024), BF16), shape((864, 512), F32)),
        in_specs=[hbm] * 4,
        out_specs=(hbm,) * 3,
        scratch_shapes=[
            pltpu.VMEM((64, 4096), BF16),
            pltpu.VMEM((2, 4, 4, 128, 128), BF16),
            pltpu.VMEM((4, 2, 16, 128), F32),
            pltpu.VMEM((32, 2, 4096), BF16),
            pltpu.VMEM((864, 512), F32),
            pltpu.SemaphoreType.DMA((14,)),
        ],
        compiler_params=pltpu.CompilerParams(vmem_limit_bytes=VMEM_MIB * 2**20),
    )(fgrad, resp, codes, run)
    return (
        resp.reshape(32, 1, 1024), fgrad, kgrad.reshape(27, 32, 512).transpose(1, 0, 2),
    )


def solution(mesh):
    in_specs = (P("chan", "depth", None), P("chan", None, None), P("chan", "depth", None))
    out_specs = (P("chan", "depth", None), P("chan", "depth", None), P("chan", None, None))
    return jax.shard_map(
        on_device, mesh=mesh, in_specs=in_specs, out_specs=out_specs, check_vma=False
    )
```

```python
import jax
import jax.numpy as jnp
from jax import lax
from jax.experimental import pallas as pl
from jax.experimental.pallas import tpu as pltpu
from jax.sharding import PartitionSpec as P

BF16 = jnp.bfloat16
F32 = jnp.float32
MESH = pl.DeviceIdType.MESH
SPAN = 250.0
MESSAGES = 136
VMEM_MIB = 56


def near(i):
    return i + 1 - 2 * (i % 2)


def far(i):
    return 3 - i


def ring_order(half):
    return (near, far) if half == 0 else (far, near)


def bound_of(values):
    rows, lanes = values.shape
    top = jnp.max(jnp.abs(values).reshape(rows // 16, 16, lanes), axis=0)
    return jnp.maximum(top, 1e-30).astype(BF16).astype(F32)


def encode(values, bound):
    rows, lanes = values.shape
    blocks = values.reshape(rows // 16, 16, lanes)
    code = jnp.exp2(jnp.abs(blocks) * (SPAN / bound)[None] - SPAN / 2)
    return jnp.where(blocks < 0, -code, code).reshape(rows, lanes).astype(BF16)


def decode(code, bound, scale=1.0):
    rows, lanes = code.shape
    blocks = code.astype(F32).reshape(rows // 16, 16, lanes)
    size = (jnp.log2(jnp.abs(blocks)) + SPAN / 2) * (bound * (scale / SPAN))[None]
    return jnp.where(blocks < 0, -size, size).reshape(rows, lanes)


def dot(a, b, dims):
    return lax.dot_general(a, b, (dims, ((), ())), preferred_element_type=F32)


def kernel(
    feat_in, kern_in, cot, resp_out, fgrad_out, kgrad_out,
    resp, fgrad, kgrad, codes, run, feat, kern, perm, patches, cells_out, cells_in, gathered, terms, spread,
    part, sy1, ry1, sy2, ry2, sz1, rz1, sz2, rz2,
    sc, rc, sx1, rx1, sx2, rx2, sz, rz, local_sem, send_sem, recv_sem,
):
    chan = lax.axis_index("chan")
    depth = lax.axis_index("depth")
    x, zl, core = chan // 4, (chan // 2) % 2, chan % 2
    zh, y = depth // 4, depth % 4
    columns = (x, near(x), far(x), near(far(x)))
    to_core = (chan + 1 - 2 * core, depth)
    to_zl = (4 * x + 2 * (1 - zl) + core, depth)
    up = (chan, (depth + 1) % 16)
    down = (chan, (depth + 15) % 16)

    def opposite(i):
        return near(far(i))

    def to_x(step):
        return (4 * step(x) + 2 * zl + core, depth)

    def to_y(step):
        return (chan, 4 * zh + step(y))

    def to_zh(step):
        return (chan, 4 * step(zh) + y)

    partners = (
        to_core, to_zl, up, down, to_x(opposite),
        to_x(near), to_x(far), to_y(near), to_y(far), to_zh(near), to_zh(far),
    )
    barrier = pltpu.get_barrier_semaphore()
    for partner in partners:
        pl.semaphore_signal(barrier, inc=1, device_id=partner, device_id_type=MESH)
    load_cot = pltpu.make_async_copy(cot, gathered.at[0, x, zl, core], local_sem.at[0])
    load_feat = pltpu.make_async_copy(feat_in, feat, local_sem.at[1])
    load_kern = pltpu.make_async_copy(kern_in, kern, local_sem.at[2])
    load_cot.start()
    load_feat.start()
    load_kern.start()

    lane_in = lax.broadcasted_iota(jnp.int32, (512, 512), 0)
    lane_out = lax.broadcasted_iota(jnp.int32, (512, 512), 1)
    target = (
        ((lane_in >> 6) & 1) * 256 + (lane_in & 1) * 128
        + (lane_in >> 7) * 32 + ((lane_in & 63) >> 1)
    )
    perm[...] = jnp.where(target == lane_out, 1.0, 0.0).astype(BF16)
    pl.semaphore_wait(barrier, len(partners))

    copies = []

    def send(src, dst, device):
        at = len(copies)
        copy = pltpu.make_async_remote_copy(
            src_ref=src, dst_ref=dst, send_sem=send_sem.at[at], recv_sem=recv_sem.at[at],
            device_id=device, device_id_type=MESH,
        )
        copy.start()
        copies.append(copy)
        return copy

    sent = {}
    steps_x = (None, near, far, opposite)

    def cot_start():
        place = gathered.at[0, x, zl, core]
        sent["z"] = send(cot, place, to_zl)
        for k in (1, 2, 3):
            sent["own", k] = send(cot, place, to_x(steps_x[k]))
        sent["core", 0] = send(cot, place, to_core)
        sent["down"] = send(cot, gathered.at[1, x, zl, core], down)

    def cot_z():
        sent["z"].wait_recv()
        place = gathered.at[0, x, 1 - zl, core]
        sent["core", 4] = send(place, place, to_core)
        for k in (1, 2, 3):
            sent["other", k] = send(place, place, to_x(steps_x[k]))

    def cot_core(k):
        sent["own", k].wait_recv()
        sent["other", k].wait_recv()
        place = gathered.at[0, columns[k], :, core]
        sent["core", k] = send(place, place, to_core)

    here = set()

    def cot_wait(k):
        if k in here:
            return
        here.add(k)
        if k == 0:
            load_cot.wait()
            sent["core", 4].wait_recv()
        sent["core", k].wait_recv()

    moves = {}

    def next_z():
        sent["down"].wait_recv()
        place = gathered.at[1, x, zl, core]
        moves["z"] = send(place, place, to_zl)

    def next_x():
        moves["z"].wait_recv()
        pair = gathered.at[1, x, :, core]
        moves["near"] = send(pair, pair, to_x(near))
        moves["far"] = send(pair, pair, to_x(far))
        moves["own_core"] = send(pair, pair, to_core)

    def next_opposite():
        moves["near"].wait_recv()
        first = gathered.at[1, near(x), :, core, 0:16]
        moves["opp0"] = send(first, first, to_x(far))
        block = gathered.at[1, near(x), :, core]
        moves["near_core"] = send(block, block, to_core)
        moves["far"].wait_recv()
        second = gathered.at[1, far(x), :, core, 16:32]
        moves["opp1"] = send(second, second, to_x(near))
        block = gathered.at[1, far(x), :, core]
        moves["far_core"] = send(block, block, to_core)

    def next_last():
        moves["opp0"].wait_recv()
        moves["opp1"].wait_recv()
        block = gathered.at[1, opposite(x), :, core]
        moves["opp_core"] = send(block, block, to_core)

    def next_wait():
        for name in ("own_core", "near_core", "far_core", "opp_core"):
            moves[name].wait_recv()

    def split_cells(plane):
        rows = feat[:, plane, :]
        stacked = jnp.concatenate([rows[:, 512 * k : 512 * k + 512] for k in range(8)], axis=0)
        sorted_cells = dot(stacked, perm[...], ((1,), (0,))).astype(BF16)
        return [
            jnp.concatenate(
                [sorted_cells[32 * k : 32 * k + 32, 128 * q : 128 * q + 128] for k in range(8)],
                axis=1,
            )
            for q in range(4)
        ]

    lane = lax.broadcasted_iota(jnp.int32, (32, 1024), 1)
    not_first_col = jnp.where((lane & 31) > 0, 1.0, 0.0).astype(BF16)
    not_first_row = jnp.where(lane >= 32, 1.0, 0.0).astype(BF16)

    def right(v):
        return pltpu.roll(v, 1, 1) * not_first_col

    def lower(v):
        return pltpu.roll(v, 32, 1) * not_first_row

    def lay_patches(a, cells):
        ee, eo, oe, oo = cells
        eo_r, oo_r = right(eo), right(oo)
        rows = (
            (lower(oo_r), lower(oe), lower(oo)),
            (eo_r, ee, eo),
            (oo_r, oe, oo),
        )
        for b in range(3):
            for c in range(3):
                at = (9 * a + 3 * b + c) * 32
                patches[at : at + 32] = rows[b][c]

    def feat_odd():
        load_feat.wait()
        cells = split_cells(1)
        for q in range(4):
            cells_out[q] = cells[q]
        sent["up"] = send(cells_out, cells_in, up)
        lay_patches(2, cells)

    def feat_even():
        lay_patches(1, split_cells(0))
        patches[864:896] = jnp.zeros((32, 1024), BF16)

    def feat_below():
        sent["up"].wait_recv()
        has_below = jnp.where(depth > 0, 1.0, 0.0).astype(BF16)
        lay_patches(0, [cells_in[q] * has_below for q in range(4)])

    grads = {}

    def grad(k, h):
        first, second = ring_order(h)
        cot_wait(k)
        weights = gathered[0, columns[k]].reshape(128, 1024)
        value = dot(patches[448 * h : 448 * h + 448], weights, ((1,), (1,)))
        for q in range(4):
            part[k, h, q, 0:112] = value[112 * q : 112 * q + 112]
        bound = bound_of(value)
        run[columns[k], h] = bound
        sy1[k, h, 0:112] = encode(part[k, h, first(y), 0:112], bound)
        sy1[k, h, 112:224] = encode(part[k, h, second(first(y)), 0:112], bound)
        sy1[k, h, 224:240] = bound.astype(BF16)
        grads[k, h] = [send(sy1.at[k, h], ry1.at[k, h], to_y(first))]

    def merge_bound(k, h, other):
        bound = jnp.maximum(run[columns[k], h], other)
        run[columns[k], h] = bound
        return bound

    def y2(k, h):
        first, second = ring_order(h)
        grads[k, h][0].wait_recv()
        other = ry1[k, h, 224:240].astype(F32)
        bound = merge_bound(k, h, other)
        part[k, h, second(y), 0:112] += decode(ry1[k, h, 112:224], other)
        sy2[k, h, 0:112] = encode(part[k, h, second(y), 0:112], 2 * bound)
        sy2[k, h, 112:128] = bound.astype(BF16)
        grads[k, h] = [send(sy2.at[k, h], ry2.at[k, h], to_y(second))]
        part[k, h, y, 0:112] += decode(ry1[k, h, 0:112], other)

    def cells_at(i):
        return pl.ds(pl.multiple_of(32 * i, 32), 32)

    def z1(k, h):
        first, second = ring_order(h)
        grads[k, h][0].wait_recv()
        other = ry2[k, h, 112:128].astype(F32)
        bound = merge_bound(k, h, other)
        part[k, h, y, 0:112] += decode(ry2[k, h, 0:112], 2 * other)
        part[k, h, y, 112:128] = jnp.zeros((16, 128), F32)
        sz1[k, h, 0:32] = encode(part[k, h, y, cells_at(first(zh))], 4 * bound)
        sz1[k, h, 32:64] = encode(part[k, h, y, cells_at(second(first(zh)))], 4 * bound)
        sz1[k, h, 64:80] = bound.astype(BF16)
        grads[k, h] = [send(sz1.at[k, h], rz1.at[k, h], to_zh(first))]

    def z2(k, h):
        first, second = ring_order(h)
        grads[k, h][0].wait_recv()
        other = rz1[k, h, 64:80].astype(F32)
        bound = merge_bound(k, h, other)
        part[k, h, y, cells_at(second(zh))] += decode(rz1[k, h, 32:64], 4 * other)
        sz2[k, h, 0:32] = encode(part[k, h, y, cells_at(second(zh))], 8 * bound)
        sz2[k, h, 32:48] = bound.astype(BF16)
        grads[k, h] = [send(sz2.at[k, h], rz2.at[k, h], to_zh(second))]
        part[k, h, y, cells_at(zh)] += decode(rz1[k, h, 0:32], 4 * other)

    def back_z1(k, h):
        first, second = ring_order(h)
        grads[k, h][0].wait_recv()
        other = rz2[k, h, 32:48].astype(F32)
        bound = merge_bound(k, h, other)
        total = part[k, h, y, cells_at(zh)] + decode(rz2[k, h, 0:32], 8 * other)
        codes[columns[k], h, y, cells_at(zh)] = encode(total, 16 * bound)
        own = codes.at[columns[k], h, y, cells_at(zh)]
        grads[k, h] = [send(own, own, to_zh(second)), send(own, own, to_zh(first))]

    def back_z2(k, h):
        first, second = ring_order(h)
        grads[k, h][0].wait_recv()
        block = codes.at[columns[k], h, y, cells_at(second(zh))]
        grads[k, h][0] = send(block, block, to_zh(first))

    def back_y1(k, h):
        first, second = ring_order(h)
        grads[k, h][0].wait_recv()
        grads[k, h][1].wait_recv()
        block = codes.at[columns[k], h, y, 0:112]
        grads[k, h] = [send(block, block, to_y(second)), send(block, block, to_y(first))]

    def back_y2(k, h):
        first, second = ring_order(h)
        grads[k, h][0].wait_recv()
        block = codes.at[columns[k], h, second(y), 0:112]
        grads[k, h][0] = send(block, block, to_y(first))

    kept = []

    def keep(src, dst):
        copy = pltpu.make_async_copy(src, dst, local_sem.at[3 + len(kept)])
        copy.start()
        kept.append(copy)

    def result(k, h):
        lanes = pl.ds(pl.multiple_of(128 * columns[k], 128), 128)
        grads[k, h][0].wait_recv()
        grads[k, h][1].wait_recv()
        bound = 16 * run[columns[k], h]
        for q in range(4):
            at = 448 * h + 112 * q
            count = min(112, 864 - at)
            kgrad[at : at + count, lanes] = decode(
                codes[columns[k], h, q, 0:count], bound, 1.0 / 128
            )
        rows = pl.ds(448 * h, 416 if h else 448)
        keep(kgrad.at[rows, lanes], kgrad_out.at[rows, lanes])

    sums = {}

    def resp_terms(i):
        if i == 0:
            load_kern.wait()
        value = dot(kern[:, 128 * i : 128 * i + 128], patches[0:864], ((0,), (0,)))
        terms[i] = value.reshape(2, 2, 32, 1024)

    def resp_core():
        bound = bound_of(terms[:, :, 1 - core].reshape(256, 1024))
        for i in range(4):
            for j in range(2):
                at = 64 * i + 32 * j
                sc[at : at + 32] = encode(terms[i, j, 1 - core], bound)
        sc[256:272] = bound.astype(BF16)
        sums["core"] = send(sc, rc, to_core)

    def resp_x1():
        sums["core"].wait_recv()
        other = rc[256:272].astype(F32)
        for i in range(4):
            for j in range(2):
                at = 64 * i + 32 * j
                terms[i, j, core] += decode(rc[at : at + 32], other)
        for h in range(2):
            first, second = ring_order(h)
            lanes = slice(512 * h, 512 * h + 512)
            blocks = [
                terms[i, j, core, :, lanes] for i in (first(x), second(first(x))) for j in range(2)
            ]
            value = jnp.concatenate(blocks, axis=0)
            bound = bound_of(value)
            sx1[h, 0:128] = encode(value, bound)
            sx1[h, 128:144] = bound.astype(BF16)
            sums["x1", h] = send(sx1.at[h], rx1.at[h], to_x(first))

    def resp_x2():
        for h in range(2):
            first, second = ring_order(h)
            lanes = slice(512 * h, 512 * h + 512)
            sums["x1", h].wait_recv()
            other = rx1[h, 128:144].astype(F32)
            for n, i in enumerate((x, second(x))):
                for j in range(2):
                    at = 64 * n + 32 * j
                    terms[i, j, core, :, lanes] += decode(rx1[h, at : at + 32], other)
            value = jnp.concatenate(
                [terms[second(x), j, core, :, lanes] for j in range(2)], axis=0
            )
            bound = bound_of(value)
            sx2[h, 0:64] = encode(value, bound)
            sx2[h, 64:80] = bound.astype(BF16)
            sums["x2", h] = send(sx2.at[h], rx2.at[h], to_x(second))

    def resp_z():
        for h in range(2):
            lanes = slice(512 * h, 512 * h + 512)
            sums["x2", h].wait_recv()
            other = rx2[h, 64:80].astype(F32)
            for j in range(2):
                terms[x, j, core, :, lanes] += decode(rx2[h, 32 * j : 32 * j + 32], other)
        value = terms[x, 1 - zl, core]
        bound = bound_of(value)
        sz[0:32] = encode(value, bound)
        sz[32:48] = bound.astype(BF16)
        sums["z"] = send(sz, rz, to_zl)

    def resp_result():
        sums["z"].wait_recv()
        total = terms[x, zl, core] + decode(rz[0:32], rz[32:48].astype(F32))
        resp[...] = total.astype(BF16)
        keep(resp, resp_out)

    not_last_col = jnp.where((lane & 31) < 31, 1.0, 0.0)
    not_last_row = jnp.where(lane < 992, 1.0, 0.0)

    def left(v):
        return pltpu.roll(v, 1023, 1) * not_last_col

    def upper(v):
        return pltpu.roll(v, 992, 1) * not_last_row

    def join_cells(plane):
        def tap(b, c):
            at = (3 * b + c) * 32
            return spread[at : at + 32]

        cells = [
            tap(1, 1),
            tap(1, 2) + left(tap(1, 0)),
            tap(2, 1) + upper(tap(0, 1)),
            tap(2, 2) + left(tap(2, 0)) + upper(tap(0, 2) + left(tap(0, 0))),
        ]
        cells = [v.astype(BF16) for v in cells]
        stacked = jnp.concatenate(
            [
                jnp.concatenate([v[:, 128 * k : 128 * k + 128] for v in cells], axis=1)
                for k in range(8)
            ],
            axis=0,
        )
        rows = dot(stacked, perm[...], ((1,), (1,))).astype(BF16)
        for k in range(8):
            fgrad[:, plane, 512 * k : 512 * k + 512] = rows[32 * k : 32 * k + 32]

    def feature_even():
        for k in range(4):
            cot_wait(k)
        cots = gathered[0].reshape(512, 1024)
        spread[...] = dot(kern[288:576], cots, ((1,), (0,)))
        join_cells(0)

    def feature_odd():
        next_wait()
        has_above = jnp.where(depth < 15, 1.0, 0.0)
        spread[...] = dot(kern[0:288], gathered[1].reshape(512, 1024), ((1,), (0,))) * has_above
        spread[...] += dot(kern[576:864], gathered[0].reshape(512, 1024), ((1,), (0,)))
        join_cells(1)
        keep(fgrad, fgrad_out)

    cot_start()
    feat_odd()
    feat_even()
    cot_z()
    grad(0, 1)
    next_z()
    cot_core(2)
    cot_core(1)
    grad(2, 1)
    grad(1, 1)
    cot_core(3)
    next_x()
    y2(0, 1)
    grad(3, 1)
    feat_below()
    grad(3, 0)
    y2(2, 1)
    grad(0, 0)
    z1(0, 1)
    grad(1, 0)
    y2(1, 1)
    resp_terms(0)
    resp_terms(1)
    resp_terms(2)
    grad(2, 0)
    y2(3, 0)
    resp_terms(3)
    z2(0, 1)
    resp_core()
    feature_even()
    y2(0, 0)
    y2(3, 1)
    next_opposite()
    z1(3, 0)
    z1(2, 1)
    y2(1, 0)
    back_z1(0, 1)
    z1(1, 1)
    resp_x1()
    z1(0, 0)
    y2(2, 0)
    z1(1, 0)
    next_last()
    z2(3, 0)
    z2(2, 1)
    z1(3, 1)
    back_z2(0, 1)
    z2(1, 1)
    z2(0, 0)
    z1(2, 0)
    back_z1(3, 0)
    z2(1, 0)
    back_z1(2, 1)
    z2(3, 1)
    resp_x2()
    back_y1(0, 1)
    back_z1(1, 1)
    back_z1(0, 0)
    z2(2, 0)
    back_z2(3, 0)
    back_z1(1, 0)
    back_z2(2, 1)
    back_y2(0, 1)
    back_z1(3, 1)
    back_z2(1, 1)
    back_z2(0, 0)
    resp_z()
    back_y1(3, 0)
    back_z1(2, 0)
    feature_odd()
    back_y1(1, 1)
    back_y1(2, 1)
    result(0, 1)
    back_y2(3, 0)
    back_y1(0, 0)
    back_z2(3, 1)
    back_z2(1, 0)
    resp_result()
    back_y2(1, 1)
    back_z2(2, 0)
    back_y2(2, 1)
    back_y1(3, 1)
    back_y1(1, 0)
    result(3, 0)
    back_y2(0, 0)
    result(1, 1)
    back_y1(2, 0)
    result(2, 1)
    back_y2(3, 1)
    back_y2(1, 0)
    result(0, 0)
    back_y2(2, 0)
    result(3, 1)
    result(1, 0)
    result(2, 0)
    for copy in copies:
        copy.wait_send()
    for copy in kept:
        copy.wait()


def finish(resp_in, fgrad_in, kgrad_in, resp, fgrad, kgrad, sem):
    copies = [
        pltpu.make_async_copy(kgrad_in, kgrad, sem.at[0]),
        pltpu.make_async_copy(fgrad_in, fgrad, sem.at[1]),
        pltpu.make_async_copy(resp_in, resp, sem.at[2]),
    ]
    for copy in copies:
        copy.start()
    for copy in copies:
        copy.wait()


def on_device(features, kernel_block, cotangent):
    kern = kernel_block.transpose(1, 0, 2).reshape(864, 512)
    cot = cotangent.reshape(32, 1024)
    shape = jax.ShapeDtypeStruct
    hbm = pl.BlockSpec(memory_space=pltpu.HBM)
    results = (shape((32, 1024), BF16), shape((32, 2, 4096), BF16), shape((864, 512), F32))
    parts = pl.pallas_call(
        kernel,
        out_shape=results,
        in_specs=[hbm] * 3,
        out_specs=(hbm,) * 3,
        scratch_shapes=[
            pltpu.VMEM((32, 1024), BF16),
            pltpu.VMEM((32, 2, 4096), BF16),
            pltpu.VMEM((864, 512), F32),
            pltpu.VMEM((4, 2, 4, 128, 128), BF16),
            pltpu.VMEM((4, 2, 16, 128), F32),
            pltpu.VMEM((32, 2, 4096), BF16),
            pltpu.VMEM((864, 512), BF16),
            pltpu.VMEM((512, 512), BF16),
            pltpu.VMEM((896, 1024), BF16),
            pltpu.VMEM((4, 32, 1024), BF16),
            pltpu.VMEM((4, 32, 1024), BF16),
            pltpu.VMEM((2, 4, 2, 2, 32, 1024), BF16),
            pltpu.VMEM((4, 2, 2, 32, 1024), F32),
            pltpu.VMEM((288, 1024), F32),
            pltpu.VMEM((4, 2, 4, 128, 128), F32),
        ]
        + [
            pltpu.VMEM((4, 2, rows, 128), BF16)
            for rows in (240, 240, 128, 128, 80, 80, 48, 48)
        ]
        + [
            pltpu.VMEM((272, 1024), BF16),
            pltpu.VMEM((272, 1024), BF16),
            pltpu.VMEM((2, 144, 512), BF16),
            pltpu.VMEM((2, 144, 512), BF16),
            pltpu.VMEM((2, 80, 512), BF16),
            pltpu.VMEM((2, 80, 512), BF16),
            pltpu.VMEM((48, 1024), BF16),
            pltpu.VMEM((48, 1024), BF16),
            pltpu.SemaphoreType.DMA((16,)),
            pltpu.SemaphoreType.DMA((MESSAGES,)),
            pltpu.SemaphoreType.DMA((MESSAGES,)),
        ],
        compiler_params=pltpu.CompilerParams(
            collective_id=0, has_side_effects=True, vmem_limit_bytes=VMEM_MIB * 2**20
        ),
    )(features, kern, cot)
    resp, fgrad, kgrad = pl.pallas_call(
        finish,
        out_shape=results,
        in_specs=[hbm] * 3,
        out_specs=(hbm,) * 3,
        scratch_shapes=[pltpu.SemaphoreType.DMA((3,))],
        compiler_params=pltpu.CompilerParams(vmem_limit_bytes=VMEM_MIB * 2**20),
    )(*parts)
    return (
        resp.reshape(32, 1, 1024), fgrad, kgrad.reshape(27, 32, 512).transpose(1, 0, 2),
    )


def solution(mesh):
    in_specs = (P("chan", "depth", None), P("chan", None, None), P("chan", "depth", None))
    out_specs = (P("chan", "depth", None), P("chan", "depth", None), P("chan", None, None))
    return jax.shard_map(
        on_device, mesh=mesh, in_specs=in_specs, out_specs=out_specs, check_vma=False
    )
```

```python
import jax
import jax.numpy as jnp
from jax import lax
from jax.experimental import pallas as pl
from jax.experimental.pallas import tpu as pltpu
from jax.sharding import PartitionSpec as P

BF16 = jnp.bfloat16
F32 = jnp.float32
MESH = pl.DeviceIdType.MESH
SPAN = 250.0
MESSAGES = 136
VMEM_MIB = 56


def near(i):
    return i + 1 - 2 * (i % 2)


def far(i):
    return 3 - i


def ring_order(half):
    return (near, far) if half == 0 else (far, near)


def bound_of(values):
    rows, lanes = values.shape
    top = jnp.max(jnp.abs(values).reshape(rows // 16, 16, lanes), axis=0)
    return jnp.maximum(top, 1e-30).astype(BF16).astype(F32)


def encode(values, bound):
    rows, lanes = values.shape
    blocks = values.reshape(rows // 16, 16, lanes)
    code = jnp.exp2(jnp.abs(blocks) * (SPAN / bound)[None] - SPAN / 2)
    return jnp.where(blocks < 0, -code, code).reshape(rows, lanes).astype(BF16)


def decode(code, bound, scale=1.0):
    rows, lanes = code.shape
    blocks = code.astype(F32).reshape(rows // 16, 16, lanes)
    size = (jnp.log2(jnp.abs(blocks)) + SPAN / 2) * (bound * (scale / SPAN))[None]
    return jnp.where(blocks < 0, -size, size).reshape(rows, lanes)


def dot(a, b, dims):
    return lax.dot_general(a, b, (dims, ((), ())), preferred_element_type=F32)


def kernel(
    feat_in, kern_in, cot, resp_out, fgrad_out, kgrad_out,
    resp, fgrad, kgrad, codes, run, feat, kern, perm, patches, cells_out, cells_in, gathered, terms, spread,
    part, sy1, ry1, sy2, ry2, sz1, rz1, sz2, rz2,
    sc, rc, sx1, rx1, sx2, rx2, sz, rz, local_sem, send_sem, recv_sem,
):
    chan = lax.axis_index("chan")
    depth = lax.axis_index("depth")
    x, zl, core = chan // 4, (chan // 2) % 2, chan % 2
    zh, y = depth // 4, depth % 4
    columns = (x, near(x), far(x), near(far(x)))
    to_core = (chan + 1 - 2 * core, depth)
    to_zl = (4 * x + 2 * (1 - zl) + core, depth)
    up = (chan, (depth + 1) % 16)
    down = (chan, (depth + 15) % 16)

    def opposite(i):
        return near(far(i))

    def to_x(step):
        return (4 * step(x) + 2 * zl + core, depth)

    def to_y(step):
        return (chan, 4 * zh + step(y))

    def to_zh(step):
        return (chan, 4 * step(zh) + y)

    partners = (
        to_core, to_zl, up, down, to_x(opposite),
        to_x(near), to_x(far), to_y(near), to_y(far), to_zh(near), to_zh(far),
    )
    barrier = pltpu.get_barrier_semaphore()
    for partner in partners:
        pl.semaphore_signal(barrier, inc=1, device_id=partner, device_id_type=MESH)
    load_cot = pltpu.make_async_copy(cot, gathered.at[0, x, zl, core], local_sem.at[0])
    load_feat = pltpu.make_async_copy(feat_in, feat, local_sem.at[1])
    load_kern = pltpu.make_async_copy(kern_in, kern, local_sem.at[2])
    load_cot.start()
    load_feat.start()
    load_kern.start()

    lane_in = lax.broadcasted_iota(jnp.int32, (512, 512), 0)
    lane_out = lax.broadcasted_iota(jnp.int32, (512, 512), 1)
    target = (
        ((lane_in >> 6) & 1) * 256 + (lane_in & 1) * 128
        + (lane_in >> 7) * 32 + ((lane_in & 63) >> 1)
    )
    perm[...] = jnp.where(target == lane_out, 1.0, 0.0).astype(BF16)
    pl.semaphore_wait(barrier, len(partners))

    copies = []

    def send(src, dst, device):
        at = len(copies)
        copy = pltpu.make_async_remote_copy(
            src_ref=src, dst_ref=dst, send_sem=send_sem.at[at], recv_sem=recv_sem.at[at],
            device_id=device, device_id_type=MESH,
        )
        copy.start()
        copies.append(copy)
        return copy

    sent = {}
    steps_x = (None, near, far, opposite)

    def cot_start():
        place = gathered.at[0, x, zl, core]
        sent["z"] = send(cot, place, to_zl)
        for k in (1, 2, 3):
            sent["own", k] = send(cot, place, to_x(steps_x[k]))
        sent["core", 0] = send(cot, place, to_core)
        sent["down"] = send(cot, gathered.at[1, x, zl, core], down)

    def cot_z():
        sent["z"].wait_recv()
        place = gathered.at[0, x, 1 - zl, core]
        sent["core", 4] = send(place, place, to_core)
        for k in (1, 2, 3):
            sent["other", k] = send(place, place, to_x(steps_x[k]))

    def cot_core(k):
        sent["own", k].wait_recv()
        sent["other", k].wait_recv()
        place = gathered.at[0, columns[k], :, core]
        sent["core", k] = send(place, place, to_core)

    here = set()

    def cot_wait(k):
        if k in here:
            return
        here.add(k)
        if k == 0:
            load_cot.wait()
            sent["core", 4].wait_recv()
        sent["core", k].wait_recv()

    moves = {}

    def next_z():
        sent["down"].wait_recv()
        place = gathered.at[1, x, zl, core]
        moves["z"] = send(place, place, to_zl)

    def next_x():
        moves["z"].wait_recv()
        pair = gathered.at[1, x, :, core]
        moves["near"] = send(pair, pair, to_x(near))
        moves["far"] = send(pair, pair, to_x(far))
        moves["own_core"] = send(pair, pair, to_core)

    def next_opposite():
        moves["near"].wait_recv()
        first = gathered.at[1, near(x), :, core, 0:16]
        moves["opp0"] = send(first, first, to_x(far))
        block = gathered.at[1, near(x), :, core]
        moves["near_core"] = send(block, block, to_core)
        moves["far"].wait_recv()
        second = gathered.at[1, far(x), :, core, 16:32]
        moves["opp1"] = send(second, second, to_x(near))
        block = gathered.at[1, far(x), :, core]
        moves["far_core"] = send(block, block, to_core)

    def next_last():
        moves["opp0"].wait_recv()
        moves["opp1"].wait_recv()
        block = gathered.at[1, opposite(x), :, core]
        moves["opp_core"] = send(block, block, to_core)

    def next_wait():
        for name in ("own_core", "near_core", "far_core", "opp_core"):
            moves[name].wait_recv()

    def split_cells(plane):
        rows = feat[:, plane, :]
        stacked = jnp.concatenate([rows[:, 512 * k : 512 * k + 512] for k in range(8)], axis=0)
        sorted_cells = dot(stacked, perm[...], ((1,), (0,))).astype(BF16)
        return [
            jnp.concatenate(
                [sorted_cells[32 * k : 32 * k + 32, 128 * q : 128 * q + 128] for k in range(8)],
                axis=1,
            )
            for q in range(4)
        ]

    lane = lax.broadcasted_iota(jnp.int32, (32, 1024), 1)
    not_first_col = jnp.where((lane & 31) > 0, 1.0, 0.0).astype(BF16)
    not_first_row = jnp.where(lane >= 32, 1.0, 0.0).astype(BF16)

    def right(v):
        return pltpu.roll(v, 1, 1) * not_first_col

    def lower(v):
        return pltpu.roll(v, 32, 1) * not_first_row

    def lay_patches(a, cells):
        ee, eo, oe, oo = cells
        eo_r, oo_r = right(eo), right(oo)
        rows = (
            (lower(oo_r), lower(oe), lower(oo)),
            (eo_r, ee, eo),
            (oo_r, oe, oo),
        )
        for b in range(3):
            for c in range(3):
                at = (9 * a + 3 * b + c) * 32
                patches[at : at + 32] = rows[b][c]

    def feat_odd():
        load_feat.wait()
        cells = split_cells(1)
        for q in range(4):
            cells_out[q] = cells[q]
        sent["up"] = send(cells_out, cells_in, up)
        lay_patches(2, cells)

    def feat_even():
        lay_patches(1, split_cells(0))
        patches[864:896] = jnp.zeros((32, 1024), BF16)

    def feat_below():
        sent["up"].wait_recv()
        has_below = jnp.where(depth > 0, 1.0, 0.0).astype(BF16)
        lay_patches(0, [cells_in[q] * has_below for q in range(4)])

    grads = {}

    def grad(k, h):
        first, second = ring_order(h)
        cot_wait(k)
        weights = gathered[0, columns[k]].reshape(128, 1024)
        value = dot(patches[448 * h : 448 * h + 448], weights, ((1,), (1,)))
        for q in range(4):
            part[k, h, q, 0:112] = value[112 * q : 112 * q + 112]
        bound = bound_of(value)
        run[columns[k], h] = bound
        sy1[k, h, 0:112] = encode(part[k, h, first(y), 0:112], bound)
        sy1[k, h, 112:224] = encode(part[k, h, second(first(y)), 0:112], bound)
        sy1[k, h, 224:240] = bound.astype(BF16)
        grads[k, h] = [send(sy1.at[k, h], ry1.at[k, h], to_y(first))]

    def merge_bound(k, h, other):
        bound = jnp.maximum(run[columns[k], h], other)
        run[columns[k], h] = bound
        return bound

    def y2(k, h):
        first, second = ring_order(h)
        grads[k, h][0].wait_recv()
        other = ry1[k, h, 224:240].astype(F32)
        bound = merge_bound(k, h, other)
        part[k, h, second(y), 0:112] += decode(ry1[k, h, 112:224], other)
        sy2[k, h, 0:112] = encode(part[k, h, second(y), 0:112], 2 * bound)
        sy2[k, h, 112:128] = bound.astype(BF16)
        grads[k, h] = [send(sy2.at[k, h], ry2.at[k, h], to_y(second))]
        part[k, h, y, 0:112] += decode(ry1[k, h, 0:112], other)

    def cells_at(i):
        return pl.ds(pl.multiple_of(32 * i, 32), 32)

    def z1(k, h):
        first, second = ring_order(h)
        grads[k, h][0].wait_recv()
        other = ry2[k, h, 112:128].astype(F32)
        bound = merge_bound(k, h, other)
        part[k, h, y, 0:112] += decode(ry2[k, h, 0:112], 2 * other)
        part[k, h, y, 112:128] = jnp.zeros((16, 128), F32)
        sz1[k, h, 0:32] = encode(part[k, h, y, cells_at(first(zh))], 4 * bound)
        sz1[k, h, 32:64] = encode(part[k, h, y, cells_at(second(first(zh)))], 4 * bound)
        sz1[k, h, 64:80] = bound.astype(BF16)
        grads[k, h] = [send(sz1.at[k, h], rz1.at[k, h], to_zh(first))]

    def z2(k, h):
        first, second = ring_order(h)
        grads[k, h][0].wait_recv()
        other = rz1[k, h, 64:80].astype(F32)
        bound = merge_bound(k, h, other)
        part[k, h, y, cells_at(second(zh))] += decode(rz1[k, h, 32:64], 4 * other)
        sz2[k, h, 0:32] = encode(part[k, h, y, cells_at(second(zh))], 8 * bound)
        sz2[k, h, 32:48] = bound.astype(BF16)
        grads[k, h] = [send(sz2.at[k, h], rz2.at[k, h], to_zh(second))]
        part[k, h, y, cells_at(zh)] += decode(rz1[k, h, 0:32], 4 * other)

    def back_z1(k, h):
        first, second = ring_order(h)
        grads[k, h][0].wait_recv()
        other = rz2[k, h, 32:48].astype(F32)
        bound = merge_bound(k, h, other)
        total = part[k, h, y, cells_at(zh)] + decode(rz2[k, h, 0:32], 8 * other)
        codes[columns[k], h, y, cells_at(zh)] = encode(total, 16 * bound)
        own = codes.at[columns[k], h, y, cells_at(zh)]
        grads[k, h] = [send(own, own, to_zh(second)), send(own, own, to_zh(first))]

    def back_z2(k, h):
        first, second = ring_order(h)
        grads[k, h][0].wait_recv()
        block = codes.at[columns[k], h, y, cells_at(second(zh))]
        grads[k, h][0] = send(block, block, to_zh(first))

    def back_y1(k, h):
        first, second = ring_order(h)
        grads[k, h][0].wait_recv()
        grads[k, h][1].wait_recv()
        block = codes.at[columns[k], h, y, 0:112]
        grads[k, h] = [send(block, block, to_y(second)), send(block, block, to_y(first))]

    def back_y2(k, h):
        first, second = ring_order(h)
        grads[k, h][0].wait_recv()
        block = codes.at[columns[k], h, second(y), 0:112]
        grads[k, h][0] = send(block, block, to_y(first))

    kept = []

    def keep(src, dst):
        copy = pltpu.make_async_copy(src, dst, local_sem.at[3 + len(kept)])
        copy.start()
        kept.append(copy)

    def result(k, h):
        lanes = pl.ds(pl.multiple_of(128 * columns[k], 128), 128)
        grads[k, h][0].wait_recv()
        grads[k, h][1].wait_recv()
        bound = 16 * run[columns[k], h]
        for q in range(4):
            at = 448 * h + 112 * q
            count = min(112, 864 - at)
            kgrad[at : at + count, lanes] = decode(
                codes[columns[k], h, q, 0:count], bound, 1.0 / 128
            )
        rows = pl.ds(448 * h, 416 if h else 448)
        keep(kgrad.at[rows, lanes], kgrad_out.at[rows, lanes])

    sums = {}

    def resp_terms(i):
        if i == 0:
            load_kern.wait()
        value = dot(kern[:, 128 * i : 128 * i + 128], patches[0:864], ((0,), (0,)))
        terms[i] = value.reshape(2, 2, 32, 1024)

    def resp_core():
        bound = bound_of(terms[:, :, 1 - core].reshape(256, 1024))
        for i in range(4):
            for j in range(2):
                at = 64 * i + 32 * j
                sc[at : at + 32] = encode(terms[i, j, 1 - core], bound)
        sc[256:272] = bound.astype(BF16)
        sums["core"] = send(sc, rc, to_core)

    def resp_x1():
        sums["core"].wait_recv()
        other = rc[256:272].astype(F32)
        for i in range(4):
            for j in range(2):
                at = 64 * i + 32 * j
                terms[i, j, core] += decode(rc[at : at + 32], other)
        for h in range(2):
            first, second = ring_order(h)
            lanes = slice(512 * h, 512 * h + 512)
            blocks = [
                terms[i, j, core, :, lanes] for i in (first(x), second(first(x))) for j in range(2)
            ]
            value = jnp.concatenate(blocks, axis=0)
            bound = bound_of(value)
            sx1[h, 0:128] = encode(value, bound)
            sx1[h, 128:144] = bound.astype(BF16)
            sums["x1", h] = send(sx1.at[h], rx1.at[h], to_x(first))

    def resp_x2():
        for h in range(2):
            first, second = ring_order(h)
            lanes = slice(512 * h, 512 * h + 512)
            sums["x1", h].wait_recv()
            other = rx1[h, 128:144].astype(F32)
            for n, i in enumerate((x, second(x))):
                for j in range(2):
                    at = 64 * n + 32 * j
                    terms[i, j, core, :, lanes] += decode(rx1[h, at : at + 32], other)
            value = jnp.concatenate(
                [terms[second(x), j, core, :, lanes] for j in range(2)], axis=0
            )
            bound = bound_of(value)
            sx2[h, 0:64] = encode(value, bound)
            sx2[h, 64:80] = bound.astype(BF16)
            sums["x2", h] = send(sx2.at[h], rx2.at[h], to_x(second))

    def resp_z():
        for h in range(2):
            lanes = slice(512 * h, 512 * h + 512)
            sums["x2", h].wait_recv()
            other = rx2[h, 64:80].astype(F32)
            for j in range(2):
                terms[x, j, core, :, lanes] += decode(rx2[h, 32 * j : 32 * j + 32], other)
        value = terms[x, 1 - zl, core]
        bound = bound_of(value)
        sz[0:32] = encode(value, bound)
        sz[32:48] = bound.astype(BF16)
        sums["z"] = send(sz, rz, to_zl)

    def resp_result():
        sums["z"].wait_recv()
        total = terms[x, zl, core] + decode(rz[0:32], rz[32:48].astype(F32))
        resp[...] = total.astype(BF16)
        keep(resp, resp_out)

    not_last_col = jnp.where((lane & 31) < 31, 1.0, 0.0)
    not_last_row = jnp.where(lane < 992, 1.0, 0.0)

    def left(v):
        return pltpu.roll(v, 1023, 1) * not_last_col

    def upper(v):
        return pltpu.roll(v, 992, 1) * not_last_row

    def join_cells(plane):
        def tap(b, c):
            at = (3 * b + c) * 32
            return spread[at : at + 32]

        cells = [
            tap(1, 1),
            tap(1, 2) + left(tap(1, 0)),
            tap(2, 1) + upper(tap(0, 1)),
            tap(2, 2) + left(tap(2, 0)) + upper(tap(0, 2) + left(tap(0, 0))),
        ]
        cells = [v.astype(BF16) for v in cells]
        stacked = jnp.concatenate(
            [
                jnp.concatenate([v[:, 128 * k : 128 * k + 128] for v in cells], axis=1)
                for k in range(8)
            ],
            axis=0,
        )
        rows = dot(stacked, perm[...], ((1,), (1,))).astype(BF16)
        for k in range(8):
            fgrad[:, plane, 512 * k : 512 * k + 512] = rows[32 * k : 32 * k + 32]

    def feature_even():
        for k in range(4):
            cot_wait(k)
        cots = gathered[0].reshape(512, 1024)
        spread[...] = dot(kern[288:576], cots, ((1,), (0,)))
        join_cells(0)

    def feature_odd():
        next_wait()
        has_above = jnp.where(depth < 15, 1.0, 0.0)
        spread[...] = dot(kern[0:288], gathered[1].reshape(512, 1024), ((1,), (0,))) * has_above
        spread[...] += dot(kern[576:864], gathered[0].reshape(512, 1024), ((1,), (0,)))
        join_cells(1)
        keep(fgrad, fgrad_out)

    cot_start()
    feat_odd()
    feat_even()
    cot_z()
    grad(0, 1)
    next_z()
    cot_core(2)
    cot_core(1)
    grad(2, 1)
    grad(1, 1)
    cot_core(3)
    y2(0, 1)
    grad(3, 1)
    next_x()
    feat_below()
    grad(1, 0)
    grad(0, 0)
    grad(3, 0)
    y2(1, 1)
    z1(0, 1)
    grad(2, 0)
    y2(2, 1)
    resp_terms(0)
    y2(3, 1)
    resp_terms(1)
    y2(1, 0)
    resp_terms(2)
    next_opposite()
    resp_terms(3)
    y2(0, 0)
    z2(0, 1)
    feature_even()
    z1(1, 0)
    y2(3, 0)
    z1(1, 1)
    z1(0, 0)
    next_last()
    back_z1(0, 1)
    y2(2, 0)
    resp_core()
    z1(3, 0)
    z1(2, 1)
    z2(1, 0)
    z1(3, 1)
    z2(1, 1)
    z2(0, 0)
    back_z2(0, 1)
    z1(2, 0)
    resp_x1()
    z2(2, 1)
    z2(3, 0)
    back_z1(1, 1)
    back_z1(1, 0)
    z2(3, 1)
    z2(2, 0)
    back_z1(0, 0)
    back_y1(0, 1)
    back_z1(2, 1)
    back_z1(3, 0)
    back_z2(1, 1)
    back_z2(1, 0)
    back_z1(3, 1)
    back_z1(2, 0)
    back_y2(0, 1)
    back_z2(0, 0)
    resp_x2()
    back_z2(2, 1)
    back_z2(3, 0)
    back_y1(1, 1)
    back_y1(1, 0)
    back_z2(3, 1)
    result(0, 1)
    back_z2(2, 0)
    back_y1(0, 0)
    back_y1(2, 1)
    back_y1(3, 0)
    back_y2(1, 1)
    resp_z()
    back_y2(1, 0)
    back_y1(3, 1)
    back_y1(2, 0)
    feature_odd()
    back_y2(0, 0)
    back_y2(3, 0)
    back_y2(2, 1)
    result(1, 1)
    result(1, 0)
    back_y2(3, 1)
    resp_result()
    back_y2(2, 0)
    result(0, 0)
    result(2, 1)
    result(3, 0)
    result(3, 1)
    result(2, 0)
    for copy in copies:
        copy.wait_send()
    for copy in kept:
        copy.wait()


def finish(resp_in, fgrad_in, kgrad_in, resp, fgrad, kgrad, resp_v, fgrad_v, kgrad_v, sem):
    parts = [(kgrad_in, kgrad_v, kgrad, pl.ds(216 * n, 216)) for n in range(4)]
    parts += [(fgrad_in, fgrad_v, fgrad, pl.ds(16 * n, 16)) for n in range(2)]
    parts += [(resp_in, resp_v, resp, pl.ds(0, 32))]
    loads, stores = [], []
    for n, (source, middle, target, rows) in enumerate(parts):
        loads.append(pltpu.make_async_copy(source.at[rows], middle.at[rows], sem.at[0, n]))
        stores.append(pltpu.make_async_copy(middle.at[rows], target.at[rows], sem.at[1, n]))
    for copy in loads:
        copy.start()
    for load, store in zip(loads, stores):
        load.wait()
        store.start()
    for copy in stores:
        copy.wait()


def on_device(features, kernel_block, cotangent):
    kern = kernel_block.transpose(1, 0, 2).reshape(864, 512)
    cot = cotangent.reshape(32, 1024)
    shape = jax.ShapeDtypeStruct
    hbm = pl.BlockSpec(memory_space=pltpu.HBM)
    results = (shape((32, 1024), BF16), shape((32, 2, 4096), BF16), shape((864, 512), F32))
    parts = pl.pallas_call(
        kernel,
        out_shape=results,
        in_specs=[hbm] * 3,
        out_specs=(hbm,) * 3,
        scratch_shapes=[
            pltpu.VMEM((32, 1024), BF16),
            pltpu.VMEM((32, 2, 4096), BF16),
            pltpu.VMEM((864, 512), F32),
            pltpu.VMEM((4, 2, 4, 128, 128), BF16),
            pltpu.VMEM((4, 2, 16, 128), F32),
            pltpu.VMEM((32, 2, 4096), BF16),
            pltpu.VMEM((864, 512), BF16),
            pltpu.VMEM((512, 512), BF16),
            pltpu.VMEM((896, 1024), BF16),
            pltpu.VMEM((4, 32, 1024), BF16),
            pltpu.VMEM((4, 32, 1024), BF16),
            pltpu.VMEM((2, 4, 2, 2, 32, 1024), BF16),
            pltpu.VMEM((4, 2, 2, 32, 1024), F32),
            pltpu.VMEM((288, 1024), F32),
            pltpu.VMEM((4, 2, 4, 128, 128), F32),
        ]
        + [
            pltpu.VMEM((4, 2, rows, 128), BF16)
            for rows in (240, 240, 128, 128, 80, 80, 48, 48)
        ]
        + [
            pltpu.VMEM((272, 1024), BF16),
            pltpu.VMEM((272, 1024), BF16),
            pltpu.VMEM((2, 144, 512), BF16),
            pltpu.VMEM((2, 144, 512), BF16),
            pltpu.VMEM((2, 80, 512), BF16),
            pltpu.VMEM((2, 80, 512), BF16),
            pltpu.VMEM((48, 1024), BF16),
            pltpu.VMEM((48, 1024), BF16),
            pltpu.SemaphoreType.DMA((16,)),
            pltpu.SemaphoreType.DMA((MESSAGES,)),
            pltpu.SemaphoreType.DMA((MESSAGES,)),
        ],
        compiler_params=pltpu.CompilerParams(
            collective_id=0, has_side_effects=True, vmem_limit_bytes=VMEM_MIB * 2**20
        ),
    )(features, kern, cot)
    resp, fgrad, kgrad = pl.pallas_call(
        finish,
        out_shape=results,
        in_specs=[hbm] * 3,
        out_specs=(hbm,) * 3,
        scratch_shapes=[
            pltpu.VMEM((32, 1024), BF16),
            pltpu.VMEM((32, 2, 4096), BF16),
            pltpu.VMEM((864, 512), F32),
            pltpu.SemaphoreType.DMA((2, 7)),
        ],
        compiler_params=pltpu.CompilerParams(vmem_limit_bytes=VMEM_MIB * 2**20),
    )(*parts)
    return (
        resp.reshape(32, 1, 1024), fgrad, kgrad.reshape(27, 32, 512).transpose(1, 0, 2),
    )


def solution(mesh):
    in_specs = (P("chan", "depth", None), P("chan", None, None), P("chan", "depth", None))
    out_specs = (P("chan", "depth", None), P("chan", "depth", None), P("chan", None, None))
    return jax.shard_map(
        on_device, mesh=mesh, in_specs=in_specs, out_specs=out_specs, check_vma=False
    )
```

```python
import jax
import jax.numpy as jnp
from jax import lax
from jax.experimental import pallas as pl
from jax.experimental.pallas import tpu as pltpu
from jax.sharding import PartitionSpec as P

BF16 = jnp.bfloat16
F32 = jnp.float32
MESH = pl.DeviceIdType.MESH
SPAN = 250.0
MESSAGES = 136
VMEM_MIB = 56


def near(i):
    return i + 1 - 2 * (i % 2)


def far(i):
    return 3 - i


def ring_order(half):
    return (near, far) if half == 0 else (far, near)


def bound_of(values):
    rows, lanes = values.shape
    top = jnp.max(jnp.abs(values).reshape(rows // 16, 16, lanes), axis=0)
    return jnp.maximum(top, 1e-30).astype(BF16).astype(F32)


def encode(values, bound):
    rows, lanes = values.shape
    blocks = values.reshape(rows // 16, 16, lanes)
    code = jnp.exp2(jnp.abs(blocks) * (SPAN / bound)[None] - SPAN / 2)
    return jnp.where(blocks < 0, -code, code).reshape(rows, lanes).astype(BF16)


def decode(code, bound, scale=1.0):
    rows, lanes = code.shape
    blocks = code.astype(F32).reshape(rows // 16, 16, lanes)
    size = (jnp.log2(jnp.abs(blocks)) + SPAN / 2) * (bound * (scale / SPAN))[None]
    return jnp.where(blocks < 0, -size, size).reshape(rows, lanes)


def dot(a, b, dims):
    return lax.dot_general(a, b, (dims, ((), ())), preferred_element_type=F32)


def kernel(
    feat_in, kern_in, cot, resp_out, fgrad_out, kgrad_out,
    resp, fgrad, kgrad, codes, run, feat, kern, perm, patches, cells_out, cells_in, gathered, terms, spread,
    part, sy1, ry1, sy2, ry2, sz1, rz1, sz2, rz2,
    sc, rc, sx1, rx1, sx2, rx2, sz, rz, local_sem, send_sem, recv_sem,
):
    chan = lax.axis_index("chan")
    depth = lax.axis_index("depth")
    x, zl, core = chan // 4, (chan // 2) % 2, chan % 2
    zh, y = depth // 4, depth % 4
    columns = (x, near(x), far(x), near(far(x)))
    to_core = (chan + 1 - 2 * core, depth)
    to_zl = (4 * x + 2 * (1 - zl) + core, depth)
    up = (chan, (depth + 1) % 16)
    down = (chan, (depth + 15) % 16)

    def opposite(i):
        return near(far(i))

    def to_x(step):
        return (4 * step(x) + 2 * zl + core, depth)

    def to_y(step):
        return (chan, 4 * zh + step(y))

    def to_zh(step):
        return (chan, 4 * step(zh) + y)

    partners = (
        to_core, to_zl, up, down, to_x(opposite),
        to_x(near), to_x(far), to_y(near), to_y(far), to_zh(near), to_zh(far),
    )
    barrier = pltpu.get_barrier_semaphore()
    for partner in partners:
        pl.semaphore_signal(barrier, inc=1, device_id=partner, device_id_type=MESH)
    load_cot = pltpu.make_async_copy(cot, gathered.at[0, x, zl, core], local_sem.at[0])
    load_feat = pltpu.make_async_copy(feat_in, feat, local_sem.at[1])
    load_kern = pltpu.make_async_copy(kern_in, kern, local_sem.at[2])
    load_cot.start()
    load_feat.start()
    load_kern.start()

    pl.semaphore_wait(barrier, len(partners))

    copies = []

    def send(src, dst, device):
        at = len(copies)
        copy = pltpu.make_async_remote_copy(
            src_ref=src, dst_ref=dst, send_sem=send_sem.at[at], recv_sem=recv_sem.at[at],
            device_id=device, device_id_type=MESH,
        )
        copy.start()
        copies.append(copy)
        return copy

    sent = {}
    steps_x = (None, near, far, opposite)

    def cot_start():
        place = gathered.at[0, x, zl, core]
        sent["z"] = send(cot, place, to_zl)
        for k in (1, 2, 3):
            sent["own", k] = send(cot, place, to_x(steps_x[k]))
        sent["core", 0] = send(cot, place, to_core)
        sent["down"] = send(cot, gathered.at[1, x, zl, core], down)

    def cot_z():
        sent["z"].wait_recv()
        place = gathered.at[0, x, 1 - zl, core]
        sent["core", 4] = send(place, place, to_core)
        for k in (1, 2, 3):
            sent["other", k] = send(place, place, to_x(steps_x[k]))

    def cot_core(k):
        sent["own", k].wait_recv()
        sent["other", k].wait_recv()
        place = gathered.at[0, columns[k], :, core]
        sent["core", k] = send(place, place, to_core)

    here = set()

    def cot_wait(k):
        if k in here:
            return
        here.add(k)
        if k == 0:
            load_cot.wait()
            sent["core", 4].wait_recv()
        sent["core", k].wait_recv()

    moves = {}

    def next_z():
        sent["down"].wait_recv()
        place = gathered.at[1, x, zl, core]
        moves["z"] = send(place, place, to_zl)

    def next_x():
        moves["z"].wait_recv()
        pair = gathered.at[1, x, :, core]
        moves["near"] = send(pair, pair, to_x(near))
        moves["far"] = send(pair, pair, to_x(far))
        moves["own_core"] = send(pair, pair, to_core)

    def next_opposite():
        moves["near"].wait_recv()
        first = gathered.at[1, near(x), :, core, 0:16]
        moves["opp0"] = send(first, first, to_x(far))
        block = gathered.at[1, near(x), :, core]
        moves["near_core"] = send(block, block, to_core)
        moves["far"].wait_recv()
        second = gathered.at[1, far(x), :, core, 16:32]
        moves["opp1"] = send(second, second, to_x(near))
        block = gathered.at[1, far(x), :, core]
        moves["far_core"] = send(block, block, to_core)

    def next_last():
        moves["opp0"].wait_recv()
        moves["opp1"].wait_recv()
        block = gathered.at[1, opposite(x), :, core]
        moves["opp_core"] = send(block, block, to_core)

    def next_wait():
        for name in ("own_core", "near_core", "far_core", "opp_core"):
            moves[name].wait_recv()

    def sort_table():
        lane_in = lax.broadcasted_iota(jnp.int32, (512, 512), 0)
        lane_out = lax.broadcasted_iota(jnp.int32, (512, 512), 1)
        target = (
            ((lane_in >> 6) & 1) * 256 + (lane_in & 1) * 128
            + (lane_in >> 7) * 32 + ((lane_in & 63) >> 1)
        )
        perm[...] = jnp.where(target == lane_out, 1.0, 0.0).astype(BF16)

    def split_cells(plane):
        rows = feat[:, plane, :]
        stacked = jnp.concatenate([rows[:, 512 * k : 512 * k + 512] for k in range(8)], axis=0)
        sorted_cells = dot(stacked, perm[...], ((1,), (0,))).astype(BF16)
        return [
            jnp.concatenate(
                [sorted_cells[32 * k : 32 * k + 32, 128 * q : 128 * q + 128] for k in range(8)],
                axis=1,
            )
            for q in range(4)
        ]

    lane = lax.broadcasted_iota(jnp.int32, (32, 1024), 1)
    not_first_col = jnp.where((lane & 31) > 0, 1.0, 0.0).astype(BF16)
    not_first_row = jnp.where(lane >= 32, 1.0, 0.0).astype(BF16)

    def right(v):
        return pltpu.roll(v, 1, 1) * not_first_col

    def lower(v):
        return pltpu.roll(v, 32, 1) * not_first_row

    def lay_patches(a, cells):
        ee, eo, oe, oo = cells
        eo_r, oo_r = right(eo), right(oo)
        rows = (
            (lower(oo_r), lower(oe), lower(oo)),
            (eo_r, ee, eo),
            (oo_r, oe, oo),
        )
        for b in range(3):
            for c in range(3):
                at = (9 * a + 3 * b + c) * 32
                patches[at : at + 32] = rows[b][c]

    def feat_odd():
        load_feat.wait()
        cells = split_cells(1)
        for q in range(4):
            cells_out[q] = cells[q]
        sent["up"] = send(cells_out, cells_in, up)
        lay_patches(2, cells)

    def feat_even():
        lay_patches(1, split_cells(0))
        patches[864:896] = jnp.zeros((32, 1024), BF16)

    def feat_below():
        sent["up"].wait_recv()
        has_below = jnp.where(depth > 0, 1.0, 0.0).astype(BF16)
        lay_patches(0, [cells_in[q] * has_below for q in range(4)])

    grads = {}

    def grad(k, h):
        first, second = ring_order(h)
        cot_wait(k)
        weights = gathered[0, columns[k]].reshape(128, 1024)
        value = dot(patches[448 * h : 448 * h + 448], weights, ((1,), (1,)))
        for q in range(4):
            part[k, h, q, 0:112] = value[112 * q : 112 * q + 112]
        bound = bound_of(value)
        run[columns[k], h] = bound
        sy1[k, h, 0:112] = encode(part[k, h, first(y), 0:112], bound)
        sy1[k, h, 112:224] = encode(part[k, h, second(first(y)), 0:112], bound)
        sy1[k, h, 224:240] = bound.astype(BF16)
        grads[k, h] = [send(sy1.at[k, h], ry1.at[k, h], to_y(first))]

    def merge_bound(k, h, other):
        bound = jnp.maximum(run[columns[k], h], other)
        run[columns[k], h] = bound
        return bound

    def y2(k, h):
        first, second = ring_order(h)
        grads[k, h][0].wait_recv()
        other = ry1[k, h, 224:240].astype(F32)
        bound = merge_bound(k, h, other)
        part[k, h, second(y), 0:112] += decode(ry1[k, h, 112:224], other)
        sy2[k, h, 0:112] = encode(part[k, h, second(y), 0:112], 2 * bound)
        sy2[k, h, 112:128] = bound.astype(BF16)
        grads[k, h] = [send(sy2.at[k, h], ry2.at[k, h], to_y(second))]
        part[k, h, y, 0:112] += decode(ry1[k, h, 0:112], other)

    def cells_at(i):
        return pl.ds(pl.multiple_of(32 * i, 32), 32)

    def z1(k, h):
        first, second = ring_order(h)
        grads[k, h][0].wait_recv()
        other = ry2[k, h, 112:128].astype(F32)
        bound = merge_bound(k, h, other)
        part[k, h, y, 0:112] += decode(ry2[k, h, 0:112], 2 * other)
        part[k, h, y, 112:128] = jnp.zeros((16, 128), F32)
        sz1[k, h, 0:32] = encode(part[k, h, y, cells_at(first(zh))], 4 * bound)
        sz1[k, h, 32:64] = encode(part[k, h, y, cells_at(second(first(zh)))], 4 * bound)
        sz1[k, h, 64:80] = bound.astype(BF16)
        grads[k, h] = [send(sz1.at[k, h], rz1.at[k, h], to_zh(first))]

    def z2(k, h):
        first, second = ring_order(h)
        grads[k, h][0].wait_recv()
        other = rz1[k, h, 64:80].astype(F32)
        bound = merge_bound(k, h, other)
        part[k, h, y, cells_at(second(zh))] += decode(rz1[k, h, 32:64], 4 * other)
        sz2[k, h, 0:32] = encode(part[k, h, y, cells_at(second(zh))], 8 * bound)
        sz2[k, h, 32:48] = bound.astype(BF16)
        grads[k, h] = [send(sz2.at[k, h], rz2.at[k, h], to_zh(second))]
        part[k, h, y, cells_at(zh)] += decode(rz1[k, h, 0:32], 4 * other)

    def back_z1(k, h):
        first, second = ring_order(h)
        grads[k, h][0].wait_recv()
        other = rz2[k, h, 32:48].astype(F32)
        bound = merge_bound(k, h, other)
        total = part[k, h, y, cells_at(zh)] + decode(rz2[k, h, 0:32], 8 * other)
        codes[columns[k], h, y, cells_at(zh)] = encode(total, 16 * bound)
        own = codes.at[columns[k], h, y, cells_at(zh)]
        grads[k, h] = [send(own, own, to_zh(second)), send(own, own, to_zh(first))]

    def back_z2(k, h):
        first, second = ring_order(h)
        grads[k, h][0].wait_recv()
        block = codes.at[columns[k], h, y, cells_at(second(zh))]
        grads[k, h][0] = send(block, block, to_zh(first))

    def back_y1(k, h):
        first, second = ring_order(h)
        grads[k, h][0].wait_recv()
        grads[k, h][1].wait_recv()
        block = codes.at[columns[k], h, y, 0:112]
        grads[k, h] = [send(block, block, to_y(second)), send(block, block, to_y(first))]

    def back_y2(k, h):
        first, second = ring_order(h)
        grads[k, h][0].wait_recv()
        block = codes.at[columns[k], h, second(y), 0:112]
        grads[k, h][0] = send(block, block, to_y(first))

    kept = []

    def keep(src, dst):
        copy = pltpu.make_async_copy(src, dst, local_sem.at[3 + len(kept)])
        copy.start()
        kept.append(copy)

    def result(k, h):
        lanes = pl.ds(pl.multiple_of(128 * columns[k], 128), 128)
        grads[k, h][0].wait_recv()
        grads[k, h][1].wait_recv()
        bound = 16 * run[columns[k], h]
        for q in range(4):
            at = 448 * h + 112 * q
            count = min(112, 864 - at)
            kgrad[at : at + count, lanes] = decode(
                codes[columns[k], h, q, 0:count], bound, 1.0 / 128
            )
        rows = pl.ds(448 * h, 416 if h else 448)
        keep(kgrad.at[rows, lanes], kgrad_out.at[rows, lanes])

    sums = {}

    def resp_terms(i):
        if i == 0:
            load_kern.wait()
        value = dot(kern[:, 128 * i : 128 * i + 128], patches[0:864], ((0,), (0,)))
        terms[i] = value.reshape(2, 2, 32, 1024)

    def resp_core():
        bound = bound_of(terms[:, :, 1 - core].reshape(256, 1024))
        for i in range(4):
            for j in range(2):
                at = 64 * i + 32 * j
                sc[at : at + 32] = encode(terms[i, j, 1 - core], bound)
        sc[256:272] = bound.astype(BF16)
        sums["core"] = send(sc, rc, to_core)

    def resp_x1():
        sums["core"].wait_recv()
        other = rc[256:272].astype(F32)
        for i in range(4):
            for j in range(2):
                at = 64 * i + 32 * j
                terms[i, j, core] += decode(rc[at : at + 32], other)
        for h in range(2):
            first, second = ring_order(h)
            lanes = slice(512 * h, 512 * h + 512)
            blocks = [
                terms[i, j, core, :, lanes] for i in (first(x), second(first(x))) for j in range(2)
            ]
            value = jnp.concatenate(blocks, axis=0)
            bound = bound_of(value)
            sx1[h, 0:128] = encode(value, bound)
            sx1[h, 128:144] = bound.astype(BF16)
            sums["x1", h] = send(sx1.at[h], rx1.at[h], to_x(first))

    def resp_x2():
        for h in range(2):
            first, second = ring_order(h)
            lanes = slice(512 * h, 512 * h + 512)
            sums["x1", h].wait_recv()
            other = rx1[h, 128:144].astype(F32)
            for n, i in enumerate((x, second(x))):
                for j in range(2):
                    at = 64 * n + 32 * j
                    terms[i, j, core, :, lanes] += decode(rx1[h, at : at + 32], other)
            value = jnp.concatenate(
                [terms[second(x), j, core, :, lanes] for j in range(2)], axis=0
            )
            bound = bound_of(value)
            sx2[h, 0:64] = encode(value, bound)
            sx2[h, 64:80] = bound.astype(BF16)
            sums["x2", h] = send(sx2.at[h], rx2.at[h], to_x(second))

    def resp_z():
        for h in range(2):
            lanes = slice(512 * h, 512 * h + 512)
            sums["x2", h].wait_recv()
            other = rx2[h, 64:80].astype(F32)
            for j in range(2):
                terms[x, j, core, :, lanes] += decode(rx2[h, 32 * j : 32 * j + 32], other)
        value = terms[x, 1 - zl, core]
        bound = bound_of(value)
        sz[0:32] = encode(value, bound)
        sz[32:48] = bound.astype(BF16)
        sums["z"] = send(sz, rz, to_zl)

    def resp_result():
        sums["z"].wait_recv()
        total = terms[x, zl, core] + decode(rz[0:32], rz[32:48].astype(F32))
        resp[...] = total.astype(BF16)
        keep(resp, resp_out)

    not_last_col = jnp.where((lane & 31) < 31, 1.0, 0.0)
    not_last_row = jnp.where(lane < 992, 1.0, 0.0)

    def left(v):
        return pltpu.roll(v, 1023, 1) * not_last_col

    def upper(v):
        return pltpu.roll(v, 992, 1) * not_last_row

    def join_cells(plane):
        def tap(b, c):
            at = (3 * b + c) * 32
            return spread[at : at + 32]

        cells = [
            tap(1, 1),
            tap(1, 2) + left(tap(1, 0)),
            tap(2, 1) + upper(tap(0, 1)),
            tap(2, 2) + left(tap(2, 0)) + upper(tap(0, 2) + left(tap(0, 0))),
        ]
        cells = [v.astype(BF16) for v in cells]
        stacked = jnp.concatenate(
            [
                jnp.concatenate([v[:, 128 * k : 128 * k + 128] for v in cells], axis=1)
                for k in range(8)
            ],
            axis=0,
        )
        rows = dot(stacked, perm[...], ((1,), (1,))).astype(BF16)
        for k in range(8):
            fgrad[:, plane, 512 * k : 512 * k + 512] = rows[32 * k : 32 * k + 32]

    def feature_even():
        for k in range(4):
            cot_wait(k)
        cots = gathered[0].reshape(512, 1024)
        spread[...] = dot(kern[288:576], cots, ((1,), (0,)))
        join_cells(0)

    def feature_odd():
        next_wait()
        has_above = jnp.where(depth < 15, 1.0, 0.0)
        spread[...] = dot(kern[0:288], gathered[1].reshape(512, 1024), ((1,), (0,))) * has_above
        spread[...] += dot(kern[576:864], gathered[0].reshape(512, 1024), ((1,), (0,)))
        join_cells(1)
        keep(fgrad, fgrad_out)

    cot_start()
    sort_table()
    feat_odd()
    feat_even()
    cot_z()
    grad(0, 1)
    next_z()
    cot_core(2)
    cot_core(1)
    grad(2, 1)
    grad(1, 1)
    cot_core(3)
    y2(0, 1)
    grad(3, 1)
    next_x()
    feat_below()
    grad(1, 0)
    grad(0, 0)
    grad(3, 0)
    y2(1, 1)
    z1(0, 1)
    grad(2, 0)
    y2(2, 1)
    resp_terms(0)
    y2(3, 1)
    resp_terms(1)
    y2(1, 0)
    resp_terms(2)
    next_opposite()
    resp_terms(3)
    y2(0, 0)
    z2(0, 1)
    feature_even()
    z1(1, 0)
    y2(3, 0)
    z1(1, 1)
    z1(0, 0)
    next_last()
    back_z1(0, 1)
    y2(2, 0)
    resp_core()
    z1(3, 0)
    z1(2, 1)
    z2(1, 0)
    z1(3, 1)
    z2(1, 1)
    z2(0, 0)
    back_z2(0, 1)
    z1(2, 0)
    resp_x1()
    z2(2, 1)
    z2(3, 0)
    back_z1(1, 1)
    back_z1(1, 0)
    z2(3, 1)
    z2(2, 0)
    back_z1(0, 0)
    back_y1(0, 1)
    back_z1(2, 1)
    back_z1(3, 0)
    back_z2(1, 1)
    back_z2(1, 0)
    back_z1(3, 1)
    back_z1(2, 0)
    back_y2(0, 1)
    back_z2(0, 0)
    resp_x2()
    back_z2(2, 1)
    back_z2(3, 0)
    back_y1(1, 1)
    back_y1(1, 0)
    back_z2(3, 1)
    result(0, 1)
    back_z2(2, 0)
    back_y1(0, 0)
    back_y1(2, 1)
    back_y1(3, 0)
    back_y2(1, 1)
    resp_z()
    back_y2(1, 0)
    back_y1(3, 1)
    back_y1(2, 0)
    feature_odd()
    back_y2(0, 0)
    back_y2(3, 0)
    back_y2(2, 1)
    result(1, 1)
    result(1, 0)
    back_y2(3, 1)
    resp_result()
    back_y2(2, 0)
    result(0, 0)
    result(2, 1)
    result(3, 0)
    result(3, 1)
    result(2, 0)
    for copy in copies:
        copy.wait_send()
    for copy in kept:
        copy.wait()


def finish(resp_in, fgrad_in, kgrad_in, resp, fgrad, kgrad, resp_v, fgrad_v, kgrad_v, sem):
    parts = [(kgrad_in, kgrad_v, kgrad, pl.ds(216 * n, 216)) for n in range(4)]
    parts += [(fgrad_in, fgrad_v, fgrad, pl.ds(16 * n, 16)) for n in range(2)]
    parts += [(resp_in, resp_v, resp, pl.ds(0, 32))]
    loads, stores = [], []
    for n, (source, middle, target, rows) in enumerate(parts):
        loads.append(pltpu.make_async_copy(source.at[rows], middle.at[rows], sem.at[0, n]))
        stores.append(pltpu.make_async_copy(middle.at[rows], target.at[rows], sem.at[1, n]))
    for copy in loads:
        copy.start()
    for load, store in zip(loads, stores):
        load.wait()
        store.start()
    for copy in stores:
        copy.wait()


def on_device(features, kernel_block, cotangent):
    kern = kernel_block.transpose(1, 0, 2).reshape(864, 512)
    cot = cotangent.reshape(32, 1024)
    shape = jax.ShapeDtypeStruct
    hbm = pl.BlockSpec(memory_space=pltpu.HBM)
    results = (shape((32, 1024), BF16), shape((32, 2, 4096), BF16), shape((864, 512), F32))
    parts = pl.pallas_call(
        kernel,
        out_shape=results,
        in_specs=[hbm] * 3,
        out_specs=(hbm,) * 3,
        scratch_shapes=[
            pltpu.VMEM((32, 1024), BF16),
            pltpu.VMEM((32, 2, 4096), BF16),
            pltpu.VMEM((864, 512), F32),
            pltpu.VMEM((4, 2, 4, 128, 128), BF16),
            pltpu.VMEM((4, 2, 16, 128), F32),
            pltpu.VMEM((32, 2, 4096), BF16),
            pltpu.VMEM((864, 512), BF16),
            pltpu.VMEM((512, 512), BF16),
            pltpu.VMEM((896, 1024), BF16),
            pltpu.VMEM((4, 32, 1024), BF16),
            pltpu.VMEM((4, 32, 1024), BF16),
            pltpu.VMEM((2, 4, 2, 2, 32, 1024), BF16),
            pltpu.VMEM((4, 2, 2, 32, 1024), F32),
            pltpu.VMEM((288, 1024), F32),
            pltpu.VMEM((4, 2, 4, 128, 128), F32),
        ]
        + [
            pltpu.VMEM((4, 2, rows, 128), BF16)
            for rows in (240, 240, 128, 128, 80, 80, 48, 48)
        ]
        + [
            pltpu.VMEM((272, 1024), BF16),
            pltpu.VMEM((272, 1024), BF16),
            pltpu.VMEM((2, 144, 512), BF16),
            pltpu.VMEM((2, 144, 512), BF16),
            pltpu.VMEM((2, 80, 512), BF16),
            pltpu.VMEM((2, 80, 512), BF16),
            pltpu.VMEM((48, 1024), BF16),
            pltpu.VMEM((48, 1024), BF16),
            pltpu.SemaphoreType.DMA((16,)),
            pltpu.SemaphoreType.DMA((MESSAGES,)),
            pltpu.SemaphoreType.DMA((MESSAGES,)),
        ],
        compiler_params=pltpu.CompilerParams(
            collective_id=0, has_side_effects=True, vmem_limit_bytes=VMEM_MIB * 2**20
        ),
    )(features, kern, cot)
    resp, fgrad, kgrad = pl.pallas_call(
        finish,
        out_shape=results,
        in_specs=[hbm] * 3,
        out_specs=(hbm,) * 3,
        scratch_shapes=[
            pltpu.VMEM((32, 1024), BF16),
            pltpu.VMEM((32, 2, 4096), BF16),
            pltpu.VMEM((864, 512), F32),
            pltpu.SemaphoreType.DMA((2, 7)),
        ],
        compiler_params=pltpu.CompilerParams(vmem_limit_bytes=VMEM_MIB * 2**20),
    )(*parts)
    return (
        resp.reshape(32, 1, 1024), fgrad, kgrad.reshape(27, 32, 512).transpose(1, 0, 2),
    )


def solution(mesh):
    in_specs = (P("chan", "depth", None), P("chan", None, None), P("chan", "depth", None))
    out_specs = (P("chan", "depth", None), P("chan", "depth", None), P("chan", None, None))
    return jax.shard_map(
        on_device, mesh=mesh, in_specs=in_specs, out_specs=out_specs, check_vma=False
    )
```

```python
import jax
import jax.numpy as jnp
from jax import lax
from jax.experimental import pallas as pl
from jax.experimental.pallas import tpu as pltpu
from jax.sharding import PartitionSpec as P

BF16 = jnp.bfloat16
F32 = jnp.float32
MESH = pl.DeviceIdType.MESH
SPAN = 250.0
MESSAGES = 136
VMEM_MIB = 56


def near(i):
    return i + 1 - 2 * (i % 2)


def far(i):
    return 3 - i


def ring_order(half):
    return (near, far) if half == 0 else (far, near)


def bound_of(values):
    rows, lanes = values.shape
    top = jnp.max(jnp.abs(values).reshape(rows // 16, 16, lanes), axis=0)
    return jnp.maximum(top, 1e-30).astype(BF16).astype(F32)


def encode(values, bound):
    rows, lanes = values.shape
    blocks = values.reshape(rows // 16, 16, lanes)
    code = jnp.exp2(jnp.abs(blocks) * (SPAN / bound)[None] - SPAN / 2)
    return jnp.where(blocks < 0, -code, code).reshape(rows, lanes).astype(BF16)


def decode(code, bound, scale=1.0):
    rows, lanes = code.shape
    blocks = code.astype(F32).reshape(rows // 16, 16, lanes)
    size = (jnp.log2(jnp.abs(blocks)) + SPAN / 2) * (bound * (scale / SPAN))[None]
    return jnp.where(blocks < 0, -size, size).reshape(rows, lanes)


def dot(a, b, dims):
    return lax.dot_general(a, b, (dims, ((), ())), preferred_element_type=F32)


def kernel(
    feat_in, kern_in, cot, resp_out, fgrad_out, kgrad_out,
    resp, fgrad, kgrad, codes, run, feat, kern, perm, patches, cells_out, cells_in, gathered, terms, spread,
    part, sy1, ry1, sy2, ry2, sz1, rz1, sz2, rz2,
    sc, rc, sx1, rx1, sx2, rx2, sz, rz, local_sem, send_sem, recv_sem,
):
    chan = lax.axis_index("chan")
    depth = lax.axis_index("depth")
    x, zl, core = chan // 4, (chan // 2) % 2, chan % 2
    zh, y = depth // 4, depth % 4
    columns = (x, near(x), far(x), near(far(x)))
    to_core = (chan + 1 - 2 * core, depth)
    to_zl = (4 * x + 2 * (1 - zl) + core, depth)
    up = (chan, (depth + 1) % 16)
    down = (chan, (depth + 15) % 16)

    def opposite(i):
        return near(far(i))

    def to_x(step):
        return (4 * step(x) + 2 * zl + core, depth)

    def to_y(step):
        return (chan, 4 * zh + step(y))

    def to_zh(step):
        return (chan, 4 * step(zh) + y)

    partners = (
        to_core, to_zl, up, down, to_x(opposite),
        to_x(near), to_x(far), to_y(near), to_y(far), to_zh(near), to_zh(far),
    )
    barrier = pltpu.get_barrier_semaphore()
    for partner in partners:
        pl.semaphore_signal(barrier, inc=1, device_id=partner, device_id_type=MESH)
    load_cot = pltpu.make_async_copy(cot, gathered.at[0, x, zl, core], local_sem.at[0])
    load_feat = pltpu.make_async_copy(feat_in, feat, local_sem.at[1])
    load_kern = pltpu.make_async_copy(kern_in, kern, local_sem.at[2])
    load_cot.start()
    load_feat.start()
    load_kern.start()

    pl.semaphore_wait(barrier, len(partners))

    copies = []

    def send(src, dst, device):
        at = len(copies)
        copy = pltpu.make_async_remote_copy(
            src_ref=src, dst_ref=dst, send_sem=send_sem.at[at], recv_sem=recv_sem.at[at],
            device_id=device, device_id_type=MESH,
        )
        copy.start()
        copies.append(copy)
        return copy

    sent = {}
    steps_x = (None, near, far, opposite)

    def cot_start():
        place = gathered.at[0, x, zl, core]
        sent["z"] = send(cot, place, to_zl)
        for k in (1, 2, 3):
            sent["own", k] = send(cot, place, to_x(steps_x[k]))
        sent["core", 0] = send(cot, place, to_core)
        sent["down"] = send(cot, gathered.at[1, x, zl, core], down)

    def cot_z():
        sent["z"].wait_recv()
        place = gathered.at[0, x, 1 - zl, core]
        sent["core", 4] = send(place, place, to_core)
        for k in (1, 2, 3):
            sent["other", k] = send(place, place, to_x(steps_x[k]))

    def cot_core(k):
        sent["own", k].wait_recv()
        sent["other", k].wait_recv()
        place = gathered.at[0, columns[k], :, core]
        sent["core", k] = send(place, place, to_core)

    here = set()

    def cot_wait(k):
        if k in here:
            return
        here.add(k)
        if k == 0:
            load_cot.wait()
            sent["core", 4].wait_recv()
        sent["core", k].wait_recv()

    moves = {}

    def next_z():
        sent["down"].wait_recv()
        place = gathered.at[1, x, zl, core]
        moves["z"] = send(place, place, to_zl)

    def next_x():
        moves["z"].wait_recv()
        pair = gathered.at[1, x, :, core]
        moves["near"] = send(pair, pair, to_x(near))
        moves["far"] = send(pair, pair, to_x(far))
        moves["own_core"] = send(pair, pair, to_core)

    def next_opposite():
        moves["near"].wait_recv()
        first = gathered.at[1, near(x), :, core, 0:16]
        moves["opp0"] = send(first, first, to_x(far))
        block = gathered.at[1, near(x), :, core]
        moves["near_core"] = send(block, block, to_core)
        moves["far"].wait_recv()
        second = gathered.at[1, far(x), :, core, 16:32]
        moves["opp1"] = send(second, second, to_x(near))
        block = gathered.at[1, far(x), :, core]
        moves["far_core"] = send(block, block, to_core)

    def next_last():
        moves["opp0"].wait_recv()
        moves["opp1"].wait_recv()
        block = gathered.at[1, opposite(x), :, core]
        moves["opp_core"] = send(block, block, to_core)

    def next_wait():
        for name in ("own_core", "near_core", "far_core", "opp_core"):
            moves[name].wait_recv()

    def sort_table():
        lane_in = lax.broadcasted_iota(jnp.int32, (512, 512), 0)
        lane_out = lax.broadcasted_iota(jnp.int32, (512, 512), 1)
        target = (
            ((lane_in >> 6) & 1) * 256 + (lane_in & 1) * 128
            + (lane_in >> 7) * 32 + ((lane_in & 63) >> 1)
        )
        perm[...] = jnp.where(target == lane_out, 1.0, 0.0).astype(BF16)

    def split_cells(plane):
        rows = feat[:, plane, :]
        stacked = jnp.concatenate([rows[:, 512 * k : 512 * k + 512] for k in range(8)], axis=0)
        sorted_cells = dot(stacked, perm[...], ((1,), (0,))).astype(BF16)
        return [
            jnp.concatenate(
                [sorted_cells[32 * k : 32 * k + 32, 128 * q : 128 * q + 128] for k in range(8)],
                axis=1,
            )
            for q in range(4)
        ]

    lane = lax.broadcasted_iota(jnp.int32, (32, 1024), 1)
    not_first_col = jnp.where((lane & 31) > 0, 1.0, 0.0).astype(BF16)
    not_first_row = jnp.where(lane >= 32, 1.0, 0.0).astype(BF16)

    def right(v):
        return pltpu.roll(v, 1, 1) * not_first_col

    def lower(v):
        return pltpu.roll(v, 32, 1) * not_first_row

    def lay_patches(a, cells):
        ee, eo, oe, oo = cells
        eo_r, oo_r = right(eo), right(oo)
        rows = (
            (lower(oo_r), lower(oe), lower(oo)),
            (eo_r, ee, eo),
            (oo_r, oe, oo),
        )
        for b in range(3):
            for c in range(3):
                at = (9 * a + 3 * b + c) * 32
                patches[at : at + 32] = rows[b][c]

    def feat_odd():
        load_feat.wait()
        cells = split_cells(1)
        for q in range(4):
            cells_out[q] = cells[q]
        sent["up"] = send(cells_out, cells_in, up)
        lay_patches(2, cells)

    def feat_even():
        lay_patches(1, split_cells(0))
        patches[864:896] = jnp.zeros((32, 1024), BF16)

    def feat_below():
        sent["up"].wait_recv()
        has_below = jnp.where(depth > 0, 1.0, 0.0).astype(BF16)
        lay_patches(0, [cells_in[q] * has_below for q in range(4)])

    grads = {}

    def grad(k, h):
        first, second = ring_order(h)
        cot_wait(k)
        weights = gathered[0, columns[k]].reshape(128, 1024)
        value = dot(patches[448 * h : 448 * h + 448], weights, ((1,), (1,)))
        for q in range(4):
            part[k, h, q, 0:112] = value[112 * q : 112 * q + 112]
        bound = bound_of(value)
        run[columns[k], h] = bound
        sy1[k, h, 0:112] = encode(part[k, h, first(y), 0:112], bound)
        sy1[k, h, 112:224] = encode(part[k, h, second(first(y)), 0:112], bound)
        sy1[k, h, 224:240] = bound.astype(BF16)
        grads[k, h] = [send(sy1.at[k, h], ry1.at[k, h], to_y(first))]

    def merge_bound(k, h, other):
        bound = jnp.maximum(run[columns[k], h], other)
        run[columns[k], h] = bound
        return bound

    def y2(k, h):
        first, second = ring_order(h)
        grads[k, h][0].wait_recv()
        other = ry1[k, h, 224:240].astype(F32)
        bound = merge_bound(k, h, other)
        part[k, h, second(y), 0:112] += decode(ry1[k, h, 112:224], other)
        sy2[k, h, 0:112] = encode(part[k, h, second(y), 0:112], 2 * bound)
        sy2[k, h, 112:128] = bound.astype(BF16)
        grads[k, h] = [send(sy2.at[k, h], ry2.at[k, h], to_y(second))]
        part[k, h, y, 0:112] += decode(ry1[k, h, 0:112], other)

    def cells_at(i):
        return pl.ds(pl.multiple_of(32 * i, 32), 32)

    def z1(k, h):
        first, second = ring_order(h)
        grads[k, h][0].wait_recv()
        other = ry2[k, h, 112:128].astype(F32)
        bound = merge_bound(k, h, other)
        part[k, h, y, 0:112] += decode(ry2[k, h, 0:112], 2 * other)
        part[k, h, y, 112:128] = jnp.zeros((16, 128), F32)
        sz1[k, h, 0:32] = encode(part[k, h, y, cells_at(first(zh))], 4 * bound)
        sz1[k, h, 32:64] = encode(part[k, h, y, cells_at(second(first(zh)))], 4 * bound)
        sz1[k, h, 64:80] = bound.astype(BF16)
        grads[k, h] = [send(sz1.at[k, h], rz1.at[k, h], to_zh(first))]

    def z2(k, h):
        first, second = ring_order(h)
        grads[k, h][0].wait_recv()
        other = rz1[k, h, 64:80].astype(F32)
        bound = merge_bound(k, h, other)
        part[k, h, y, cells_at(second(zh))] += decode(rz1[k, h, 32:64], 4 * other)
        sz2[k, h, 0:32] = encode(part[k, h, y, cells_at(second(zh))], 8 * bound)
        sz2[k, h, 32:48] = bound.astype(BF16)
        grads[k, h] = [send(sz2.at[k, h], rz2.at[k, h], to_zh(second))]
        part[k, h, y, cells_at(zh)] += decode(rz1[k, h, 0:32], 4 * other)

    def back_z1(k, h):
        first, second = ring_order(h)
        grads[k, h][0].wait_recv()
        other = rz2[k, h, 32:48].astype(F32)
        bound = merge_bound(k, h, other)
        total = part[k, h, y, cells_at(zh)] + decode(rz2[k, h, 0:32], 8 * other)
        codes[columns[k], h, y, cells_at(zh)] = encode(total, 16 * bound)
        own = codes.at[columns[k], h, y, cells_at(zh)]
        grads[k, h] = [send(own, own, to_zh(second)), send(own, own, to_zh(first))]

    def back_z2(k, h):
        first, second = ring_order(h)
        grads[k, h][0].wait_recv()
        block = codes.at[columns[k], h, y, cells_at(second(zh))]
        grads[k, h][0] = send(block, block, to_zh(first))

    def back_y1(k, h):
        first, second = ring_order(h)
        grads[k, h][0].wait_recv()
        grads[k, h][1].wait_recv()
        block = codes.at[columns[k], h, y, 0:112]
        grads[k, h] = [send(block, block, to_y(second)), send(block, block, to_y(first))]

    def back_y2(k, h):
        first, second = ring_order(h)
        grads[k, h][0].wait_recv()
        block = codes.at[columns[k], h, second(y), 0:112]
        grads[k, h][0] = send(block, block, to_y(first))

    kept = []

    def keep(src, dst):
        copy = pltpu.make_async_copy(src, dst, local_sem.at[3 + len(kept)])
        copy.start()
        kept.append(copy)

    def result(k, h):
        lanes = pl.ds(pl.multiple_of(128 * columns[k], 128), 128)
        grads[k, h][0].wait_recv()
        grads[k, h][1].wait_recv()
        bound = 16 * run[columns[k], h]
        for q in range(4):
            at = 448 * h + 112 * q
            count = min(112, 864 - at)
            kgrad[at : at + count, lanes] = decode(
                codes[columns[k], h, q, 0:count], bound, 1.0 / 128
            )
        rows = pl.ds(448 * h, 416 if h else 448)
        keep(kgrad.at[rows, lanes], kgrad_out.at[rows, lanes])

    sums = {}

    def resp_terms(i):
        if i == 0:
            load_kern.wait()
        value = dot(kern[:, 128 * i : 128 * i + 128], patches[0:864], ((0,), (0,)))
        terms[i] = value.reshape(2, 2, 32, 1024)

    def resp_core():
        bound = bound_of(terms[:, :, 1 - core].reshape(256, 1024))
        for i in range(4):
            for j in range(2):
                at = 64 * i + 32 * j
                sc[at : at + 32] = encode(terms[i, j, 1 - core], bound)
        sc[256:272] = bound.astype(BF16)
        sums["core"] = send(sc, rc, to_core)

    def resp_x1():
        sums["core"].wait_recv()
        other = rc[256:272].astype(F32)
        for i in range(4):
            for j in range(2):
                at = 64 * i + 32 * j
                terms[i, j, core] += decode(rc[at : at + 32], other)
        for h in range(2):
            first, second = ring_order(h)
            lanes = slice(512 * h, 512 * h + 512)
            blocks = [
                terms[i, j, core, :, lanes] for i in (first(x), second(first(x))) for j in range(2)
            ]
            value = jnp.concatenate(blocks, axis=0)
            bound = bound_of(value)
            sx1[h, 0:128] = encode(value, bound)
            sx1[h, 128:144] = bound.astype(BF16)
            sums["x1", h] = send(sx1.at[h], rx1.at[h], to_x(first))

    def resp_x2():
        for h in range(2):
            first, second = ring_order(h)
            lanes = slice(512 * h, 512 * h + 512)
            sums["x1", h].wait_recv()
            other = rx1[h, 128:144].astype(F32)
            for n, i in enumerate((x, second(x))):
                for j in range(2):
                    at = 64 * n + 32 * j
                    terms[i, j, core, :, lanes] += decode(rx1[h, at : at + 32], other)
            value = jnp.concatenate(
                [terms[second(x), j, core, :, lanes] for j in range(2)], axis=0
            )
            bound = bound_of(value)
            sx2[h, 0:64] = encode(value, bound)
            sx2[h, 64:80] = bound.astype(BF16)
            sums["x2", h] = send(sx2.at[h], rx2.at[h], to_x(second))

    def resp_z():
        for h in range(2):
            lanes = slice(512 * h, 512 * h + 512)
            sums["x2", h].wait_recv()
            other = rx2[h, 64:80].astype(F32)
            for j in range(2):
                terms[x, j, core, :, lanes] += decode(rx2[h, 32 * j : 32 * j + 32], other)
        value = terms[x, 1 - zl, core]
        bound = bound_of(value)
        sz[0:32] = encode(value, bound)
        sz[32:48] = bound.astype(BF16)
        sums["z"] = send(sz, rz, to_zl)

    def resp_result():
        sums["z"].wait_recv()
        total = terms[x, zl, core] + decode(rz[0:32], rz[32:48].astype(F32))
        resp[...] = total.astype(BF16)
        keep(resp, resp_out)

    not_last_col = jnp.where((lane & 31) < 31, 1.0, 0.0)
    not_last_row = jnp.where(lane < 992, 1.0, 0.0)

    def left(v):
        return pltpu.roll(v, 1023, 1) * not_last_col

    def upper(v):
        return pltpu.roll(v, 992, 1) * not_last_row

    def join_cells(plane):
        def tap(b, c):
            at = (3 * b + c) * 32
            return spread[at : at + 32]

        cells = [
            tap(1, 1),
            tap(1, 2) + left(tap(1, 0)),
            tap(2, 1) + upper(tap(0, 1)),
            tap(2, 2) + left(tap(2, 0)) + upper(tap(0, 2) + left(tap(0, 0))),
        ]
        cells = [v.astype(BF16) for v in cells]
        stacked = jnp.concatenate(
            [
                jnp.concatenate([v[:, 128 * k : 128 * k + 128] for v in cells], axis=1)
                for k in range(8)
            ],
            axis=0,
        )
        rows = dot(stacked, perm[...], ((1,), (1,))).astype(BF16)
        for k in range(8):
            fgrad[:, plane, 512 * k : 512 * k + 512] = rows[32 * k : 32 * k + 32]

    def feature_even():
        for k in range(4):
            cot_wait(k)
        cots = gathered[0].reshape(512, 1024)
        spread[...] = dot(kern[288:576], cots, ((1,), (0,)))
        join_cells(0)

    def feature_odd():
        next_wait()
        has_above = jnp.where(depth < 15, 1.0, 0.0)
        spread[...] = dot(kern[0:288], gathered[1].reshape(512, 1024), ((1,), (0,))) * has_above
        spread[...] += dot(kern[576:864], gathered[0].reshape(512, 1024), ((1,), (0,)))
        join_cells(1)
        keep(fgrad, fgrad_out)

    cot_start()
    sort_table()
    feat_odd()
    feat_even()
    cot_z()
    grad(0, 1)
    next_z()
    cot_core(2)
    cot_core(1)
    grad(2, 1)
    grad(1, 1)
    cot_core(3)
    y2(0, 1)
    grad(3, 1)
    next_x()
    feat_below()
    grad(1, 0)
    grad(0, 0)
    grad(3, 0)
    y2(1, 1)
    z1(0, 1)
    grad(2, 0)
    y2(2, 1)
    resp_terms(0)
    y2(3, 1)
    resp_terms(1)
    y2(1, 0)
    resp_terms(2)
    next_opposite()
    resp_terms(3)
    y2(0, 0)
    z2(0, 1)
    feature_even()
    z1(1, 0)
    y2(3, 0)
    z1(1, 1)
    z1(0, 0)
    next_last()
    back_z1(0, 1)
    y2(2, 0)
    resp_core()
    z1(3, 0)
    z1(2, 1)
    z2(1, 0)
    z1(3, 1)
    z2(1, 1)
    z2(0, 0)
    back_z2(0, 1)
    z1(2, 0)
    resp_x1()
    z2(2, 1)
    z2(3, 0)
    back_z1(1, 1)
    back_z1(1, 0)
    z2(3, 1)
    z2(2, 0)
    back_z1(0, 0)
    back_y1(0, 1)
    back_z1(2, 1)
    back_z1(3, 0)
    back_z2(1, 1)
    back_z2(1, 0)
    back_z1(3, 1)
    back_z1(2, 0)
    back_y2(0, 1)
    back_z2(0, 0)
    resp_x2()
    back_z2(2, 1)
    back_z2(3, 0)
    back_y1(1, 1)
    back_y1(1, 0)
    back_z2(3, 1)
    result(0, 1)
    back_z2(2, 0)
    back_y1(0, 0)
    back_y1(2, 1)
    back_y1(3, 0)
    back_y2(1, 1)
    resp_z()
    back_y2(1, 0)
    back_y1(3, 1)
    back_y1(2, 0)
    feature_odd()
    back_y2(0, 0)
    back_y2(3, 0)
    back_y2(2, 1)
    result(1, 1)
    result(1, 0)
    back_y2(3, 1)
    resp_result()
    back_y2(2, 0)
    result(0, 0)
    result(2, 1)
    result(3, 0)
    result(3, 1)
    result(2, 0)
    for copy in copies:
        copy.wait_send()
    for copy in kept:
        copy.wait()


def finish(resp_in, fgrad_in, kgrad_in, resp, fgrad, kgrad, resp_v, fgrad_v, kgrad_v, sem):
    parts = [(kgrad_in, kgrad_v, kgrad, pl.ds(96 * n, 96)) for n in range(9)]
    parts += [(fgrad_in, fgrad_v, fgrad, pl.ds(16 * n, 16)) for n in range(2)]
    parts += [(resp_in, resp_v, resp, pl.ds(0, 32))]
    loads, stores = [], []
    for n, (source, middle, target, rows) in enumerate(parts):
        loads.append(pltpu.make_async_copy(source.at[rows], middle.at[rows], sem.at[0, n]))
        stores.append(pltpu.make_async_copy(middle.at[rows], target.at[rows], sem.at[1, n]))
    for copy in loads:
        copy.start()
    for load, store in zip(loads, stores):
        load.wait()
        store.start()
    for copy in stores:
        copy.wait()


def on_device(features, kernel_block, cotangent):
    kern = kernel_block.transpose(1, 0, 2).reshape(864, 512)
    cot = cotangent.reshape(32, 1024)
    shape = jax.ShapeDtypeStruct
    hbm = pl.BlockSpec(memory_space=pltpu.HBM)
    results = (shape((32, 1024), BF16), shape((32, 2, 4096), BF16), shape((864, 512), F32))
    parts = pl.pallas_call(
        kernel,
        out_shape=results,
        in_specs=[hbm] * 3,
        out_specs=(hbm,) * 3,
        scratch_shapes=[
            pltpu.VMEM((32, 1024), BF16),
            pltpu.VMEM((32, 2, 4096), BF16),
            pltpu.VMEM((864, 512), F32),
            pltpu.VMEM((4, 2, 4, 128, 128), BF16),
            pltpu.VMEM((4, 2, 16, 128), F32),
            pltpu.VMEM((32, 2, 4096), BF16),
            pltpu.VMEM((864, 512), BF16),
            pltpu.VMEM((512, 512), BF16),
            pltpu.VMEM((896, 1024), BF16),
            pltpu.VMEM((4, 32, 1024), BF16),
            pltpu.VMEM((4, 32, 1024), BF16),
            pltpu.VMEM((2, 4, 2, 2, 32, 1024), BF16),
            pltpu.VMEM((4, 2, 2, 32, 1024), F32),
            pltpu.VMEM((288, 1024), F32),
            pltpu.VMEM((4, 2, 4, 128, 128), F32),
        ]
        + [
            pltpu.VMEM((4, 2, rows, 128), BF16)
            for rows in (240, 240, 128, 128, 80, 80, 48, 48)
        ]
        + [
            pltpu.VMEM((272, 1024), BF16),
            pltpu.VMEM((272, 1024), BF16),
            pltpu.VMEM((2, 144, 512), BF16),
            pltpu.VMEM((2, 144, 512), BF16),
            pltpu.VMEM((2, 80, 512), BF16),
            pltpu.VMEM((2, 80, 512), BF16),
            pltpu.VMEM((48, 1024), BF16),
            pltpu.VMEM((48, 1024), BF16),
            pltpu.SemaphoreType.DMA((16,)),
            pltpu.SemaphoreType.DMA((MESSAGES,)),
            pltpu.SemaphoreType.DMA((MESSAGES,)),
        ],
        compiler_params=pltpu.CompilerParams(
            collective_id=0, has_side_effects=True, vmem_limit_bytes=VMEM_MIB * 2**20
        ),
    )(features, kern, cot)
    resp, fgrad, kgrad = pl.pallas_call(
        finish,
        out_shape=results,
        in_specs=[hbm] * 3,
        out_specs=(hbm,) * 3,
        scratch_shapes=[
            pltpu.VMEM((32, 1024), BF16),
            pltpu.VMEM((32, 2, 4096), BF16),
            pltpu.VMEM((864, 512), F32),
            pltpu.SemaphoreType.DMA((2, 12)),
        ],
        compiler_params=pltpu.CompilerParams(vmem_limit_bytes=VMEM_MIB * 2**20),
    )(*parts)
    return (
        resp.reshape(32, 1, 1024), fgrad, kgrad.reshape(27, 32, 512).transpose(1, 0, 2),
    )


def solution(mesh):
    in_specs = (P("chan", "depth", None), P("chan", None, None), P("chan", "depth", None))
    out_specs = (P("chan", "depth", None), P("chan", "depth", None), P("chan", None, None))
    return jax.shard_map(
        on_device, mesh=mesh, in_specs=in_specs, out_specs=out_specs, check_vma=False
    )
```
